256 devices in a mesh: dp: 32 (over z, y), section: 8 (over x, core).
Axes of the slice: x: 4, y: 4, z: 8, core: 2. Of those that a mesh axis runs over, the one named last changes fastest.
Arguments:
- final_hidden: bfloat16 [4, 128, 5376], P(None, 'dp', 'section'), may hold values from -64 to 64
- out_weight: bfloat16 [131072, 5376], P(('dp', 'section')), may hold values from -0.25 to 0.25
- targets: int32 [4, 128], replicated, may hold values from 0 to 131071
- token_weight: float32 [4, 128], replicated, may hold values from 0.25 to 4
Outputs:
- loss: float32 [4, 128], replicated
- grad_hidden: bfloat16 [4, 128, 5376], P(None, 'dp', 'section')
- grad_weight: bfloat16 [131072, 5376], P(('dp', 'section'))
The draws below stay inside these ranges and needn't reach their ends.
All inputs are finite; a program needn't handle non-finite values.
Results may differ from the reference program's by a relative error of at most 0.0047.
Values may be sent and summed in bfloat16 or wider, within the bound.
A program may use at most 128 MiB of HBM per device.

```python
import math
import jax
import jax.numpy as jnp
from jax import lax

D = 5376
VOC_DEV = 512
MICRO = 4
VOCAB = 131072
BATCH_ROWS = 128


def shared_table(key):
    base = jax.random.normal(jax.random.fold_in(key, 5), (VOCAB, D), jnp.float32) * (3.0 / math.sqrt(D))
    return jnp.clip(base, -0.25, 0.25)


def draw_out_weight(key, part):
    vocab_table = shared_table(key)
    return vocab_table.astype(jnp.bfloat16)


def draw_final_hidden(key, part):
    vocab_table = shared_table(key).astype(jnp.bfloat16).astype(jnp.float32)
    key = jax.random.fold_in(key, 2)
    keys_list = jax.random.split(key, 8)
    drawn_rows = jnp.clip(jax.random.normal(keys_list[0], (MICRO, BATCH_ROWS, D), jnp.float32), -5.0, 5.0)
    scattered = jax.random.randint(keys_list[2], (MICRO, BATCH_ROWS), 0, 16) == 0
    forced = jax.random.randint(keys_list[6], (MICRO, 1), 0, BATCH_ROWS)
    row_ids = jnp.arange(BATCH_ROWS, dtype=jnp.int32)[None, :]
    chosen = jnp.logical_or(scattered, row_ids == forced)
    earlier = jax.random.randint(keys_list[3], (MICRO, BATCH_ROWS), 0, VOCAB)
    later = (earlier + jax.random.randint(keys_list[4], (MICRO, BATCH_ROWS), 1, VOCAB)) % VOCAB
    strength = jax.random.uniform(keys_list[5], (MICRO, BATCH_ROWS, 1), jnp.float32, 220.0, 300.0)
    offset = jax.random.uniform(keys_list[7], (MICRO, BATCH_ROWS, 1), jnp.float32, 1.0, 3.0)
    first_rows = vocab_table[earlier]
    second_rows = vocab_table[later]
    first_norm = jnp.sum(first_rows * first_rows, axis=-1, keepdims=True)
    second_norm = jnp.sum(second_rows * second_rows, axis=-1, keepdims=True)
    aligned = strength * first_rows / first_norm + (strength - offset) * second_rows / second_norm
    result_rows = jnp.where(chosen[:, :, None], aligned, drawn_rows)
    return jnp.clip(result_rows, -64.0, 64.0).astype(jnp.bfloat16)


def set_ends(values, own_key, smallest, high):
    place = [jax.random.randint(jax.random.fold_in(own_key, axis), (), 0, length) for axis, length in enumerate(values.shape)]
    main_axis = values.shape.index(max(values.shape))
    next_to = place[:main_axis] + [(place[main_axis] + 1) % values.shape[main_axis]] + place[main_axis + 1:]
    return values.at[tuple(place)].set(smallest).at[tuple(next_to)].set(high)


def setup_inputs(seed: int = 0) -> dict:
    splits = jax.random.split(jax.random.key(seed), 5)
    return {
        "final_hidden": draw_final_hidden(jax.random.fold_in(splits[4], 71), 0),
        "out_weight": draw_out_weight(jax.random.fold_in(splits[4], 71), 0),
        "targets": set_ends(jax.random.randint(splits[2], (MICRO, BATCH_ROWS), 0, VOCAB), jax.random.fold_in(splits[2], 1), 0, VOCAB - 1).astype(jnp.int32),
        "token_weight": jnp.clip(jnp.exp(jax.random.uniform(splits[3], (MICRO, BATCH_ROWS), jnp.float32, math.log(0.25), math.log(4.0))), 0.25, 4.0),
    }


def reference(final_hidden, out_weight, targets, token_weight):
    micro_count = final_hidden.shape[0]
    batch_rows = final_hidden.shape[1]
    token_rows = final_hidden.reshape(-1, D)
    logits = lax.dot_general(token_rows, out_weight, (((1,), (1,)), ((), ())), preferred_element_type=jnp.float32)
    highest = lax.optimization_barrier(jnp.max(logits, axis=1))
    summed = lax.optimization_barrier(jnp.sum(jnp.exp(logits - highest[:, None]), axis=1))
    log_norm = highest + jnp.log(summed)
    vocab_ids = jnp.arange(VOCAB, dtype=jnp.int32)
    matches = vocab_ids[None, :] == targets.reshape(-1).astype(jnp.int32)[:, None]
    picked = lax.optimization_barrier(jnp.sum(jnp.where(matches, logits, 0.0), axis=1))
    loss = (log_norm - picked).reshape(micro_count, batch_rows)
    logit_grads = (token_weight.reshape(-1)[:, None] * (jnp.exp(logits - log_norm[:, None]) - matches.astype(jnp.float32))).astype(jnp.bfloat16)
    grad_hidden = jnp.dot(logit_grads, out_weight, preferred_element_type=jnp.float32).astype(jnp.bfloat16).reshape(micro_count, batch_rows, D)
    grad_blocks = logit_grads.reshape(-1, VOCAB // VOC_DEV, VOC_DEV).transpose(1, 0, 2)

    def block_grad(block):
        return lax.dot_general(block, token_rows, (((0,), (0,)), ((), ())), preferred_element_type=jnp.float32).astype(jnp.bfloat16)
    grad_weight = lax.map(block_grad, grad_blocks).reshape(VOCAB, D)
    return (loss, grad_hidden, grad_weight)
```

```python
import functools

import jax
import jax.numpy as jnp
from jax import lax
from jax.experimental import pallas as pl
from jax.experimental.pallas import tpu as pltpu
from jax.sharding import PartitionSpec as P

MESH = pl.DeviceIdType.MESH
F32, BF16 = jnp.float32, jnp.bfloat16
NX, NY, NZ = 4, 4, 8
FRAME = 768
L0, L1, L2 = 384, 256, 128
OFF0, OFF1, OFF2 = 0, L0, L0 + L1


def frame_tile(section):
    return (21 * section) // 4


def kernel(
    h_ref, w_hbm, tgt_ref, tw_ref,
    loss_ref, gh_ref, gw_hbm,
    w, h, lt, p, pt, gw, pad, mine,
    a0, a1, a2,
    gs, rc, s0, s1, s2, r0, r1, r2, t0, t1, t2, q0, q1, q2, c0, c1, c2, d0, d1, d2,
    st1, st2,
    w_sem, gw_sem,
    ag_s, ag_r, f0_s, f0_r, f1_s, f1_r, f2_s, f2_r, st_s, st_r,
    gc_s, gc_r, rs_s, rs_r,
):
    dp = lax.axis_index("dp")
    section = lax.axis_index("section")
    z, y = dp // NY, dp % NY
    x, c = section // 2, section % 2

    def at(dz=0, dy=0, dx=0, dc=0):
        return (
            lax.rem(z + dz, NZ) * NY + lax.rem(y + dy, NY),
            lax.rem(x + dx, NX) * 2 + lax.rem(c + dc, 2),
        )

    sibling = at(dc=1)

    load_w = pltpu.make_async_copy(w_hbm, w, w_sem)
    load_w.start()

    plane = [(k // NX, k % NX) for k in range(1, NX * NY)]
    column = [(k // 2, k % 2) for k in range(1, NZ * 2)]
    barrier = pltpu.get_barrier_semaphore()
    for dy, dx in plane:
        pl.semaphore_signal(barrier, inc=1, device_id=at(dy=dy, dx=dx), device_id_type=MESH)
    for dz, dc in column:
        pl.semaphore_signal(barrier, inc=1, device_id=at(dz=dz, dc=dc), device_id_type=MESH)

    pad[...] = jnp.zeros_like(pad)
    for m in range(4):
        pad[4 * m : 4 * m + 4, 0:672] = h_ref[m].astype(F32)
    shift = lax.rem(section, 4) * 32
    framed = pltpu.roll(pad[...], shift, axis=1).astype(BF16)
    a0[c, x, z, y] = framed[:, OFF0 : OFF0 + L0]
    a1[c, x, z, y] = framed[:, OFF1 : OFF1 + L1]
    a2[c, x, z, y] = framed[:, OFF2 : OFF2 + L2]

    pl.semaphore_wait(barrier, len(plane) + len(column))

    sends = []

    def send(src, dst, s_sem, r_sem, device):
        copy = pltpu.make_async_remote_copy(
            src_ref=src, dst_ref=dst, send_sem=s_sem, recv_sem=r_sem,
            device_id=device, device_id_type=MESH,
        )
        copy.start()
        sends.append(copy)
        return copy

    slot = iter(range(1000))

    def gather(ref, axis, n):
        out = []
        for o in range(1, n):
            k = next(slot)
            out.append(send(ref, ref, ag_s.at[k], ag_r.at[k], at(**{"d" + axis: o})))
        return out

    def arrive(copies):
        for copy in copies:
            copy.wait_recv()

    e0 = gather(a0.at[c, x, z, y], "z", NZ)
    e1 = gather(a1.at[c, x, z, y], "z", NZ)
    e2 = gather(a2.at[c, x, z, y], "x", NX)
    arrive(e2)
    e2 = gather(a2.at[c, :, z, y], "y", NY)
    arrive(e0)
    e0 = gather(a0.at[c, x, :, y], "y", NY)
    arrive(e1)
    e1 = gather(a1.at[c, x, :, y], "x", NX)
    arrive(e2)
    e2 = gather(a2.at[c, :, z], "z", NZ)
    send(a2.at[c, :, z], a2.at[c, :, z], f2_s.at[0], f2_r.at[0], sibling)
    arrive(e0)
    e0 = gather(a0.at[c, x], "x", NX)
    send(a0.at[c, x], a0.at[c, x], f0_s.at[0], f0_r.at[0], sibling)
    arrive(e1)
    e1 = gather(a1.at[c, :, :, y], "y", NY)
    send(a1.at[c, :, :, y], a1.at[c, :, :, y], f1_s.at[0], f1_r.at[0], sibling)
    for o in range(1, NZ):
        e2[o - 1].wait_recv()
        part = a2.at[c, :, lax.rem(z + NZ - o, NZ)]
        send(part, part, f2_s.at[o], f2_r.at[o], sibling)
    for o in range(1, NY):
        e1[o - 1].wait_recv()
        part = a1.at[c, :, :, lax.rem(y + NY - o, NY)]
        send(part, part, f1_s.at[o], f1_r.at[o], sibling)
    for o in range(1, NX):
        e0[o - 1].wait_recv()
        part = a0.at[c, lax.rem(x + NX - o, NX)]
        send(part, part, f0_s.at[o], f0_r.at[o], sibling)

    def landed(ref, s_sem, r_sem):
        pltpu.make_async_remote_copy(
            src_ref=ref, dst_ref=ref, send_sem=s_sem, recv_sem=r_sem,
            device_id=sibling, device_id_type=MESH,
        ).wait_recv()

    other = 1 - c
    for o in range(NZ):
        landed(a2.at[other, :, lax.rem(z + NZ - o, NZ)], f2_s.at[o], f2_r.at[o])
    for o in range(NY):
        landed(a1.at[other, :, :, lax.rem(y + NY - o, NY)], f1_s.at[o], f1_r.at[o])
    for o in range(NX):
        landed(a0.at[other, lax.rem(x + NX - o, NX)], f0_s.at[o], f0_r.at[o])

    def frame_part(s, tile, zz):
        lane = tile * 128
        for buf, off, width in ((a0, OFF0, L0), (a1, OFF1, L1), (a2, OFF2, L2)):
            if off <= lane < off + width:
                v = buf[s % 2, s // 2, zz, :, :, lane - off : lane - off + 128]
                return v.reshape(NY * 16, 128)

    def assemble(zz, carry):
        rows = pl.ds(pl.multiple_of(zz * 64, 64), 64)
        for tile in range(42):
            v = None
            for s in range(8):
                if frame_tile(s) <= tile < frame_tile(s) + 6:
                    part = frame_part(s, tile - frame_tile(s), zz)
                    v = part if v is None else v + part
            h[rows, tile * 128 : tile * 128 + 128] = v
        return carry

    lax.fori_loop(0, NZ, assemble, 0)

    load_w.wait()
    lt[...] = jnp.zeros_like(lt)

    def logits_step(k, carry):
        cols = pl.ds(pl.multiple_of(k * 768, 768), 768)
        lt[...] += lax.dot_general(
            w[:, cols], h[:, cols], (((1,), (1,)), ((), ())), preferred_element_type=F32
        )
        return carry

    lax.fori_loop(0, 7, logits_step, 0)

    first_id = (dp * (NX * 2) + section) * 512
    ids = first_id + lax.broadcasted_iota(jnp.int32, (512, 512), 0)
    logits = lt[...]
    matches = ids == tgt_ref[...]
    picked = jnp.sum(jnp.where(matches, logits, 0.0), axis=0, keepdims=True)
    top = jnp.max(logits, axis=0, keepdims=True)
    lse = top + jnp.log(jnp.sum(jnp.exp(logits - top), axis=0, keepdims=True))
    for i in range(4):
        st1[0, i : i + 1, :] = lse[:, i * 128 : i * 128 + 128]
        st1[0, 4 + i : 5 + i, :] = picked[:, i * 128 : i * 128 + 128]

    def combine(buf):
        v = buf[...]
        m = jnp.max(v[:, 0:4], axis=0)
        total = m + jnp.log(jnp.sum(jnp.exp(v[:, 0:4] - m[None]), axis=0))
        return total, jnp.sum(v[:, 4:8], axis=0)

    around = []
    for k, (dy, dx) in enumerate(plane):
        around.append(send(st1.at[0], st1.at[k + 1], st_s.at[k], st_r.at[k], at(dy=dy, dx=dx)))
    arrive(around)
    total, hit = combine(st1)
    st2[0, 0:4, :] = total
    st2[0, 4:8, :] = hit
    around = []
    for k, (dz, dc) in enumerate(column):
        around.append(
            send(st2.at[0], st2.at[k + 1], st_s.at[15 + k], st_r.at[15 + k], at(dz=dz, dc=dc))
        )
    arrive(around)
    log_norm, hit = combine(st2)
    loss_ref[...] = log_norm - hit
    norm_row = jnp.concatenate([log_norm[i : i + 1] for i in range(4)], axis=1)

    for b in range(4):
        rows = slice(b * 128, b * 128 + 128)
        hot = first_id + b * 128 + lax.broadcasted_iota(jnp.int32, (128, 512), 0) == tgt_ref[...]
        g = tw_ref[...] * (jnp.exp(lt[rows, :] - norm_row) - hot.astype(F32))
        pt[rows, :] = g.astype(BF16)
        p[:, rows] = jnp.transpose(g).astype(BF16)

    def share(s):
        cols = pl.ds(pl.multiple_of(frame_tile(s) * 128, 128), FRAME)
        return lax.dot_general(
            p[...], w[:, cols], (((1,), (0,)), ((), ())), preferred_element_type=F32
        )

    def core_copy(xx):
        return pltpu.make_async_remote_copy(
            src_ref=gs.at[xx], dst_ref=rc.at[xx], send_sem=gc_s.at[xx], recv_sem=gc_r.at[xx],
            device_id=sibling, device_id_type=MESH,
        )

    def for_sibling(xx, carry):
        gs[xx] = share(xx * 2 + other).astype(BF16)
        core_copy(xx).start()
        return carry

    lax.fori_loop(0, NX, for_sibling, 0)

    def for_me(xx, carry):
        mine[...] = share(xx * 2 + c)
        core_copy(xx).wait_recv()
        for zz in range(NZ):
            v = mine[zz * 64 : zz * 64 + 64, :] + rc[xx, zz * 64 : zz * 64 + 64, :].astype(F32)
            v = v.astype(BF16)
            s0[xx, zz] = v[:, OFF0 : OFF0 + L0].reshape(NY, 16, L0)
            for yy in range(NY):
                s1[yy, xx, zz] = v[yy * 16 : yy * 16 + 16, OFF1 : OFF1 + L1]
            s2[zz, xx] = v[:, OFF2 : OFF2 + L2].reshape(NY, 16, L2)
        return carry

    lax.fori_loop(0, NX, for_me, 0)

    def scatter(src, dst, axis, n, index):
        out = []
        for o in range(1, n):
            k = next(slot)
            out.append(
                send(
                    src.at[lax.rem(index + o, n)], dst.at[o - 1],
                    rs_s.at[k - AG_COPIES], rs_r.at[k - AG_COPIES], at(**{"d" + axis: o}),
                )
            )
        return out

    e2 = scatter(s2, r2, "z", NZ, z)
    e0 = scatter(s0, r0, "x", NX, x)
    e1 = scatter(s1, r1, "y", NY, y)

    def weight_step(k, carry):
        cols = pl.ds(pl.multiple_of(k * 768, 768), 768)
        gw[:, cols] = lax.dot_general(
            pt[...], h[:, cols], (((1,), (0,)), ((), ())), preferred_element_type=F32
        ).astype(BF16)
        return carry

    lax.fori_loop(0, 7, weight_step, 0)
    store_gw = pltpu.make_async_copy(gw, gw_hbm, gw_sem)
    store_gw.start()

    def reduced(own, got, n):
        total = own.astype(F32)
        for o in range(n - 1):
            total = total + got(o).astype(F32)
        return total

    arrive(e2)
    for xx in range(NX):
        t2[xx] = reduced(s2[z, xx], lambda o: r2[o, xx], NZ).astype(BF16)
    e2 = scatter(t2, q2, "x", NX, x)
    arrive(e1)

    def sum1(xx, carry):
        t1[xx] = reduced(s1[y, xx], lambda o: r1[o, xx], NY).astype(BF16)
        return carry

    lax.fori_loop(0, NX, sum1, 0)
    e1 = scatter(t1, q1, "x", NX, x)
    arrive(e0)

    def sum0(zz, carry):
        v = reduced(s0[x, zz], lambda o: r0[o, zz], NX).astype(BF16)
        for yy in range(NY):
            t0[yy, zz] = v[yy]
        return carry

    lax.fori_loop(0, NZ, sum0, 0)
    e0 = scatter(t0, q0, "y", NY, y)

    arrive(e2)
    c2[...] = reduced(t2[x], lambda o: q2[o], NX)
    e2 = scatter(c2, d2, "y", NY, y)
    arrive(e1)
    c1[...] = reduced(t1[x], lambda o: q1[o], NX)
    e1 = scatter(c1, d1, "z", NZ, z)
    arrive(e0)
    c0[...] = reduced(t0[y], lambda o: q0[o], NY)
    e0 = scatter(c0, d0, "z", NZ, z)
    arrive(e2)
    pad[:, OFF2 : OFF2 + L2] = reduced(c2[y], lambda o: d2[o], NY)
    arrive(e1)
    pad[:, OFF1 : OFF1 + L1] = reduced(c1[z], lambda o: d1[o], NZ)
    arrive(e0)
    pad[:, OFF0 : OFF0 + L0] = reduced(c0[z], lambda o: d0[o], NZ)
    pad[...] = pltpu.roll(pad[...], lax.rem(FRAME - shift, FRAME), axis=1)
    for m in range(4):
        gh_ref[m] = pad[4 * m : 4 * m + 4, 0:672].astype(BF16)

    for copy in sends:
        copy.wait_send()

    def sent(xx, carry):
        core_copy(xx).wait_send()
        return carry

    lax.fori_loop(0, NX, sent, 0)
    store_gw.wait()


AG_COPIES = (NZ - 1) * 3 + (NX - 1) * 3 + (NY - 1) * 3
RS_COPIES = AG_COPIES


def per_device(final_hidden, out_weight, targets, token_weight):
    def order(v):
        return v.reshape(4, 32, 4).transpose(1, 0, 2).reshape(1, 512)

    vm, dma = pltpu.VMEM, pltpu.SemaphoreType.DMA
    scratch = [
        vm((512, 5376), BF16),
        vm((512, 5376), BF16),
        vm((512, 512), F32),
        vm((512, 512), BF16),
        vm((512, 512), BF16),
        vm((512, 5376), BF16),
        vm((16, FRAME), F32),
        vm((512, FRAME), F32),
        vm((2, NX, NZ, NY, 16, L0), BF16),
        vm((2, NX, NZ, NY, 16, L1), BF16),
        vm((2, NX, NZ, NY, 16, L2), BF16),
        vm((NX, 512, FRAME), BF16),
        vm((NX, 512, FRAME), BF16),
        vm((NX, NZ, NY, 16, L0), BF16),
        vm((NY, NX, NZ, 16, L1), BF16),
        vm((NZ, NX, NY, 16, L2), BF16),
        vm((NX - 1, NZ, NY, 16, L0), BF16),
        vm((NY - 1, NX, NZ, 16, L1), BF16),
        vm((NZ - 1, NX, NY, 16, L2), BF16),
        vm((NY, NZ, 16, L0), BF16),
        vm((NX, NZ, 16, L1), BF16),
        vm((NX, NY, 16, L2), BF16),
        vm((NY - 1, NZ, 16, L0), BF16),
        vm((NX - 1, NZ, 16, L1), BF16),
        vm((NX - 1, NY, 16, L2), BF16),
        vm((NZ, 16, L0), F32),
        vm((NZ, 16, L1), F32),
        vm((NY, 16, L2), F32),
        vm((NZ - 1, 16, L0), F32),
        vm((NZ - 1, 16, L1), F32),
        vm((NY - 1, 16, L2), F32),
        vm((16, 8, 128), F32),
        vm((16, 8, 128), F32),
        dma, dma,
        dma((AG_COPIES,)), dma((AG_COPIES,)),
        dma((NX,)), dma((NX,)), dma((NY,)), dma((NY,)), dma((NZ,)), dma((NZ,)),
        dma((30,)), dma((30,)),
        dma((NX,)), dma((NX,)),
        dma((RS_COPIES,)), dma((RS_COPIES,)),
    ]
    vmem = pl.BlockSpec(memory_space=pltpu.VMEM)
    hbm = pl.BlockSpec(memory_space=pl.ANY)
    loss, grad_hidden, grad_weight = pl.pallas_call(
        kernel,
        out_shape=(
            jax.ShapeDtypeStruct((4, 128), F32),
            jax.ShapeDtypeStruct((4, 4, 672), BF16),
            jax.ShapeDtypeStruct((512, 5376), BF16),
        ),
        in_specs=[vmem, hbm, vmem, vmem],
        out_specs=(vmem, vmem, hbm),
        scratch_shapes=scratch,
        compiler_params=pltpu.CompilerParams(
            collective_id=0, has_side_effects=True, vmem_limit_bytes=60 * 2**20
        ),
        name="xent",
    )(final_hidden, out_weight, order(targets), order(token_weight))
    loss = loss.reshape(32, 4, 4).transpose(1, 0, 2).reshape(4, 128)
    return (loss, grad_hidden, grad_weight)


def solution(mesh):
    in_specs = (P(None, "dp", "section"), P(("dp", "section"), None), P(), P())
    out_specs = (P(), P(None, "dp", "section"), P(("dp", "section"), None))
    return jax.shard_map(
        per_device, mesh=mesh, in_specs=in_specs, out_specs=out_specs, check_vma=False
    )
```

```python
import heapq

import jax
import jax.numpy as jnp
from jax import lax
from jax.experimental import pallas as pl
from jax.experimental.pallas import tpu as pltpu
from jax.sharding import PartitionSpec as P

MESH = pl.DeviceIdType.MESH
F32, BF16 = jnp.float32, jnp.bfloat16
NX, NY, NZ = 4, 4, 8
FRAME = 768
LANES = 256
REL = (2, 1, 3, 0)
COPIES = 200


def frame_tile(section):
    return (21 * section) // 4


def run_by_time(*tasks):
    heap = []
    for k, (start, task) in enumerate(tasks):
        heapq.heappush(heap, (start, k, task))
    while heap:
        _, k, task = heapq.heappop(heap)
        try:
            heapq.heappush(heap, (next(task), k, task))
        except StopIteration:
            pass


def pieces(v):
    hi = v.astype(BF16).astype(F32)
    mid = (v - hi).astype(BF16).astype(F32)
    return hi, mid, v - hi - mid


def kernel(
    h_ref, w_hbm, tgt_ref, tw_ref,
    loss_ref, gh_ref, h, pt,
    w, lt, p, pad, mine, rows, tgt, tw,
    a0, a1, a2,
    gs, rc, s0, s1, s2, u0a, u0b, l0, m0, u1a, u1b, l1, m1, l2, m2,
    t0, t1, t2, q0, q1, q2, c0, c1, c2, d0, d1, d2,
    st1, st2,
    w_sem, send_sem, recv_sem,
):
    dp = lax.axis_index("dp")
    section = lax.axis_index("section")
    z, y = dp // NY, dp % NY
    x, c = section // 2, section % 2
    other = 1 - c

    def at(dz=0, dy=0, dx=0, dc=0):
        return (
            lax.rem(z + dz, NZ) * NY + lax.rem(y + dy, NY),
            lax.rem(x + dx, NX) * 2 + lax.rem(c + dc, 2),
        )

    def zo(o):
        return lax.rem(z + o + NZ, NZ)

    def yo(o):
        return lax.rem(y + o + NY, NY)

    def xo(o):
        return lax.rem(x + o + NX, NX)

    sibling = at(dc=1)
    x_right, x_left = at(dx=1), at(dx=3)
    y_right, y_left = at(dy=1), at(dy=3)
    z_right, z_left = at(dz=1), at(dz=7)

    load_w = pltpu.make_async_copy(w_hbm, w, w_sem)
    load_w.start()

    plane = [(k // NX, k % NX) for k in range(1, NX * NY)]
    column = [(k // 2, k % 2) for k in range(1, NZ * 2)]
    barrier = pltpu.get_barrier_semaphore()
    for dy, dx in plane:
        pl.semaphore_signal(barrier, inc=1, device_id=at(dy=dy, dx=dx), device_id_type=MESH)
    for dz, dc in column:
        pl.semaphore_signal(barrier, inc=1, device_id=at(dz=dz, dc=dc), device_id_type=MESH)

    pad[...] = jnp.zeros_like(pad)
    for m in range(4):
        pad[4 * m : 4 * m + 4, 0:672] = h_ref[m].astype(F32)
    shift = lax.rem(section, 4) * 32
    framed = pltpu.roll(pad[...], shift, axis=1).astype(BF16)
    a0[c, x, z, y] = framed[:, 0:256]
    a1[c, x, z, y] = framed[:, 256:512]
    a2[c, x, z, y] = framed[:, 512:768]

    pl.semaphore_wait(barrier, len(plane) + len(column))

    sends = []

    def send(src, dst, device):
        k = len(sends)
        copy = pltpu.make_async_remote_copy(
            src_ref=src, dst_ref=dst, send_sem=send_sem.at[k], recv_sem=recv_sem.at[k],
            device_id=device, device_id_type=MESH,
        )
        copy.start()
        sends.append(copy)
        return copy

    def arrive(copies):
        for copy in copies:
            copy.wait_recv()

    def gather(ref, axis, n):
        return [send(ref, ref, at(**{"d" + axis: o})) for o in range(1, n)]

    from_sibling = []

    def pass_on(ref):
        from_sibling.append(send(ref, ref, sibling))

    def gather0():
        e = gather(a0.at[c, x, z, y], "z", NZ)
        yield 5.0
        arrive(e)
        e = gather(a0.at[c, x, :, y], "y", NY)
        yield 9.0
        arrive(e)
        up, down = pl.ds(0, 4), pl.ds(4, 4)
        own_up, own_down = a0.at[c, x, up], a0.at[c, x, down]
        ru = send(own_up, own_up, x_right)
        ld = send(own_down, own_down, x_left)
        rd = send(own_down, own_down, x_right)
        lu = send(own_up, own_up, x_left)
        pass_on(a0.at[c, x])
        yield 13.5
        ru.wait_recv()
        part = a0.at[c, xo(-1), up]
        fu = send(part, part, x_right)
        ld.wait_recv()
        part = a0.at[c, xo(1), down]
        fd = send(part, part, x_left)
        yield 16.5
        rd.wait_recv()
        pass_on(a0.at[c, xo(-1)])
        lu.wait_recv()
        pass_on(a0.at[c, xo(1)])
        yield 19.5
        fu.wait_recv()
        pass_on(a0.at[c, xo(2), up])
        fd.wait_recv()
        pass_on(a0.at[c, xo(2), down])

    def gather1():
        e = gather(a1.at[c, x, z, y], "z", NZ)
        yield 5.1
        arrive(e)
        e = gather(a1.at[c, x, :, y], "x", NX)
        yield 9.1
        arrive(e)

        def part(o, half):
            return a1.at[c, pl.ds(2 * half, 2), :, yo(o)]

        ru = send(part(0, 0), part(0, 0), y_right)
        ld = send(part(0, 1), part(0, 1), y_left)
        rd = send(part(0, 1), part(0, 1), y_right)
        lu = send(part(0, 0), part(0, 0), y_left)
        pass_on(a1.at[c, :, :, y])
        yield 13.6
        ru.wait_recv()
        fu = send(part(-1, 0), part(-1, 0), y_right)
        ld.wait_recv()
        fd = send(part(1, 1), part(1, 1), y_left)
        yield 16.6
        rd.wait_recv()
        pass_on(a1.at[c, :, :, yo(-1)])
        lu.wait_recv()
        pass_on(a1.at[c, :, :, yo(1)])
        yield 19.6
        fu.wait_recv()
        pass_on(part(2, 0))
        fd.wait_recv()
        pass_on(part(2, 1))

    def gather2():
        e = gather(a2.at[c, x, z, y], "x", NX)
        yield 3.0
        arrive(e)
        e = gather(a2.at[c, :, z, y], "y", NY)
        yield 6.0
        arrive(e)
        right, left = [], []
        for i in range(NX):
            part = a2.at[c, i, z]
            right.append(send(part, part, z_right))
            left.append(send(part, part, z_left))
        pass_on(a2.at[c, :, z])
        for k in range(1, NZ // 2):
            for i in range(NX):
                yield 6.0 + 2.75 * k + 0.7 * i
                right[i].wait_recv()
                if k < 3 or i < 2:
                    part = a2.at[c, i, zo(-k)]
                    right[i] = send(part, part, z_right)
                left[i].wait_recv()
                if k < 3 or i >= 2:
                    part = a2.at[c, i, zo(k)]
                    left[i] = send(part, part, z_left)
            pass_on(a2.at[c, :, zo(-k)])
            pass_on(a2.at[c, :, zo(k)])
        yield 19.7
        arrive(right[:2])
        pass_on(a2.at[c, pl.ds(0, 2), zo(4)])
        arrive(left[2:])
        pass_on(a2.at[c, pl.ds(2, 2), zo(4)])

    def token_order():
        yield 1.0
        t = tgt_ref[...]
        parts = [(t & 63).astype(F32), ((t >> 6) & 63).astype(F32), (t >> 12).astype(F32)]
        parts += list(pieces(tw_ref[...]))
        for i in range(6):
            for m in range(4):
                rows[m, i : i + 1, :] = parts[i][m : m + 1, :]
        yield 1.5
        src = lax.broadcasted_iota(jnp.int32, (128, 512), 0)
        dst = lax.broadcasted_iota(jnp.int32, (128, 512), 1)
        out = jnp.zeros((8, 512), F32)
        for m in range(4):
            hot = dst == (src // 4) * 16 + m * 4 + src % 4
            out += jnp.dot(
                rows[m].astype(BF16), hot.astype(BF16), preferred_element_type=F32
            )
        number = out[0:1].astype(jnp.int32) + out[1:2].astype(jnp.int32) * 64
        tgt[...] = number + out[2:3].astype(jnp.int32) * 4096
        tw[...] = out[3:4] + out[4:5] + out[5:6]

    rows[...] = jnp.zeros_like(rows)
    run_by_time((0.0, gather0()), (0.0, gather1()), (0.0, gather2()), (1.0, token_order()))
    arrive(from_sibling)
    load_w.wait()

    for s in range(8):
        acc = None
        for j, buf in enumerate((a0, a1, a2)):
            lane = frame_tile(s) * 128 + j * LANES
            v = lax.dot_general(
                w[:, lane : lane + LANES], buf[s % 2, s // 2].reshape(512, LANES),
                (((1,), (1,)), ((), ())), preferred_element_type=F32,
            )
            acc = v if acc is None else acc + v
        if s == 0:
            lt[...] = acc
        else:
            lt[...] += acc

    first_id = (dp * (NX * 2) + section) * 512
    ids = first_id + lax.broadcasted_iota(jnp.int32, (512, 512), 0)
    logits = lt[...]
    picked = jnp.sum(jnp.where(ids == tgt[...], logits, 0.0), axis=0, keepdims=True)
    top = jnp.max(logits, axis=0, keepdims=True)
    lse = top + jnp.log(jnp.sum(jnp.exp(logits - top), axis=0, keepdims=True))
    for i in range(4):
        st1[0, i : i + 1, :] = lse[:, i * 128 : i * 128 + 128]
        st1[0, 4 + i : 5 + i, :] = picked[:, i * 128 : i * 128 + 128]

    def combine(buf):
        v = buf[...]
        m = jnp.max(v[:, 0:4], axis=0)
        total = m + jnp.log(jnp.sum(jnp.exp(v[:, 0:4] - m[None]), axis=0))
        return total, jnp.sum(v[:, 4:8], axis=0)

    def frame_part(s, tile, zz):
        buf = (a0, a1, a2)[tile // 2]
        lane = (tile % 2) * 128
        return buf[s % 2, s // 2, zz, :, :, lane : lane + 128].reshape(NY * 16, 128)

    def assemble(zz, carry):
        dst = pl.ds(pl.multiple_of(zz * 64, 64), 64)
        for tile in range(42):
            v = None
            for s in range(8):
                if frame_tile(s) <= tile < frame_tile(s) + 6:
                    part = frame_part(s, tile - frame_tile(s), zz)
                    v = part if v is None else v + part
            h[dst, tile * 128 : tile * 128 + 128] = v
        return carry

    around = [send(st1.at[0], st1.at[k + 1], at(dy=d[0], dx=d[1])) for k, d in enumerate(plane)]
    lax.fori_loop(0, NZ // 2, assemble, 0)
    arrive(around)
    total, hit = combine(st1)
    st2[0, 0:4, :] = total
    st2[0, 4:8, :] = hit
    around = [send(st2.at[0], st2.at[k + 1], at(dz=d[0], dc=d[1])) for k, d in enumerate(column)]
    lax.fori_loop(NZ // 2, NZ, assemble, 0)
    arrive(around)
    log_norm, hit = combine(st2)
    norm_row = jnp.concatenate([log_norm[i : i + 1] for i in range(4)], axis=1)

    for b in range(4):
        r = slice(b * 128, b * 128 + 128)
        hot = first_id + b * 128 + lax.broadcasted_iota(jnp.int32, (128, 512), 0) == tgt[...]
        g = tw[...] * (jnp.exp(lt[r, :] - norm_row) - hot.astype(F32))
        pt[r, :] = g.astype(BF16)
        p[:, r] = jnp.transpose(g).astype(BF16)

    def share(s):
        cols = pl.ds(pl.multiple_of(frame_tile(s) * 128, 128), FRAME)
        return lax.dot_general(
            p[...], w[:, cols], (((1,), (0,)), ((), ())), preferred_element_type=F32
        )

    core = []
    for i, o in enumerate(REL):
        gs[i] = share(xo(o) * 2 + other).astype(BF16)
        core.append(send(gs.at[i], rc.at[i], sibling))

    def add_core(i):
        mine[...] = share(xo(REL[i]) * 2 + c)
        core[i].wait_recv()
        for zz in range(NZ):
            r = slice(zz * 64, zz * 64 + 64)
            v = (mine[r, :] + rc[i, r, :].astype(F32)).astype(BF16)
            s0[i, zz] = v[:, 0:256].reshape(NY, 16, LANES)
            for yy in range(NY):
                s1[yy, i, zz] = v[yy * 16 : yy * 16 + 16, 256:512]
            s2[zz, i] = v[:, 512:768].reshape(NY, 16, LANES)

    up, down = pl.ds(0, 4), pl.ds(4, 4)
    up_slice, down_slice = slice(0, 4), slice(4, 8)
    ring0 = {}

    def scatter0():
        yield 6.0
        ring0["ua"].wait_recv()
        s0[1, up_slice] = (s0[1, up_slice].astype(F32) + u0a[...].astype(F32)).astype(BF16)
        ring0["ra"] = send(s0.at[1, up], l0.at[up], x_right)
        ring0["ub"].wait_recv()
        s0[2, down_slice] = (s0[2, down_slice].astype(F32) + u0b[...].astype(F32)).astype(BF16)
        ring0["lb"] = send(s0.at[2, down], m0.at[down], x_left)
        yield 13.0
        arrive([ring0["ra"], ring0["rb"], ring0["la"], ring0["lb"]])
        for zz in range(NZ):
            v = s0[3, zz].astype(F32) + l0[zz].astype(F32) + m0[zz].astype(F32)
            v = v.astype(BF16)
            for yy in range(NY):
                t0[yy, zz] = v[yy]
        e = [send(t0.at[yo(o)], q0.at[o - 1], at(dy=o)) for o in range(1, NY)]
        yield 18.0
        arrive(e)
        c0[...] = sum([q0[k].astype(F32) for k in range(NY - 1)], t0[y].astype(F32))
        e = [send(c0.at[zo(o)], d0.at[o - 1], at(dz=o)) for o in range(1, NZ)]
        yield 23.0
        arrive(e)
        pad[:, 0:256] = sum([d0[k] for k in range(NZ - 1)], c0[z])

    ring1 = {}

    def scatter1():
        yield 7.5
        ring1["ua"].wait_recv()
        r = yo(1)
        s1[r, 0:2] = (s1[r, 0:2].astype(F32) + u1a[...].astype(F32)).astype(BF16)
        ring1["ra"] = send(s1.at[r, pl.ds(0, 2)], l1.at[pl.ds(0, 2)], y_right)
        ring1["ub"].wait_recv()
        r = yo(-1)
        s1[r, 2:4] = (s1[r, 2:4].astype(F32) + u1b[...].astype(F32)).astype(BF16)
        ring1["lb"] = send(s1.at[r, pl.ds(2, 2)], m1.at[pl.ds(2, 2)], y_left)
        yield 13.1
        arrive([ring1["ra"], ring1["rb"], ring1["la"], ring1["lb"]])
        for i in range(NX):
            v = s1[y, i].astype(F32) + l1[i].astype(F32) + m1[i].astype(F32)
            t1[i] = v.astype(BF16)
        e = [send(t1.at[REL.index(o)], q1.at[o - 1], at(dx=o)) for o in range(1, NX)]
        yield 18.1
        arrive(e)
        c1[...] = sum([q1[k].astype(F32) for k in range(NX - 1)], t1[3].astype(F32))
        e = [send(c1.at[zo(o)], d1.at[o - 1], at(dz=o)) for o in range(1, NZ)]
        yield 23.1
        arrive(e)
        pad[:, 256:512] = sum([d1[k] for k in range(NZ - 1)], c1[z])

    right, left = {}, {}

    def scatter2():
        for k in range(1, 4):
            for i in range(NX):
                yield 3.0 + 2.75 * k + 0.7 * i
                if k > 1 or i < 2:
                    right[k, i].wait_recv()
                    r = zo(4 - k)
                    s2[r, i] = (s2[r, i].astype(F32) + l2[k - 1, i].astype(F32)).astype(BF16)
                    right[k + 1, i] = send(s2.at[r, i], l2.at[k, i], z_right)
                if k > 1 or i >= 2:
                    left[k, i].wait_recv()
                    r = zo(k - 4)
                    s2[r, i] = (s2[r, i].astype(F32) + m2[k - 1, i].astype(F32)).astype(BF16)
                    left[k + 1, i] = send(s2.at[r, i], m2.at[k, i], z_left)
        for i in range(NX):
            yield 3.0 + 2.75 * 4 + 0.7 * i
            right[4, i].wait_recv()
            left[4, i].wait_recv()
            v = s2[z, i].astype(F32) + l2[3, i].astype(F32) + m2[3, i].astype(F32)
            t2[i] = v.astype(BF16)
        e = [send(t2.at[REL.index(o)], q2.at[o - 1], at(dx=o)) for o in range(1, NX)]
        yield 20.0
        arrive(e)
        c2[...] = sum([q2[k].astype(F32) for k in range(NX - 1)], t2[3].astype(F32))
        e = [send(c2.at[yo(o)], d2.at[o - 1], at(dy=o)) for o in range(1, NY)]
        yield 23.2
        arrive(e)
        pad[:, 512:768] = sum([d2[k] for k in range(NY - 1)], c2[y])

    for i in range(NX):
        add_core(i)
        if i == 0:
            ring0["ua"] = send(s0.at[0, up], u0a, x_right)
            ring0["ub"] = send(s0.at[0, down], u0b, x_left)
        if i == 1:
            ring0["rb"] = send(s0.at[1, down], l0.at[down], x_right)
        if i == 2:
            ring0["la"] = send(s0.at[2, up], m0.at[up], x_left)
        if i < 2:
            right[1, i] = send(s2.at[zo(4), i], l2.at[0, i], z_right)
            left[2, i] = send(s2.at[zo(-3), i], m2.at[1, i], z_left)
        else:
            left[1, i] = send(s2.at[zo(4), i], m2.at[0, i], z_left)
            right[2, i] = send(s2.at[zo(3), i], l2.at[1, i], z_right)
        if i == 1:
            ring1["ua"] = send(s1.at[yo(2), pl.ds(0, 2)], u1a, y_right)
            ring1["la"] = send(s1.at[yo(-1), pl.ds(0, 2)], m1.at[pl.ds(0, 2)], y_left)
        if i == 3:
            ring1["ub"] = send(s1.at[yo(2), pl.ds(2, 2)], u1b, y_left)
            ring1["rb"] = send(s1.at[yo(1), pl.ds(2, 2)], l1.at[pl.ds(2, 2)], y_right)

    def loss_order():
        yield 12.0
        rows[...] = jnp.zeros_like(rows)
        for i, v in enumerate(pieces(log_norm - hit)):
            rows[i, 0:4, :] = v
        yield 12.5
        src = lax.broadcasted_iota(jnp.int32, (128, 128), 0)
        dst = lax.broadcasted_iota(jnp.int32, (128, 128), 1)
        pick = lax.broadcasted_iota(jnp.int32, (8, 128), 0) == (
            lax.broadcasted_iota(jnp.int32, (8, 128), 1) // 32
        )
        for m in range(4):
            hot = (src == ((dst // 4) % 8) * 16 + m * 4 + dst % 4).astype(BF16)
            v = sum(
                jnp.dot(rows[i].astype(BF16), hot, preferred_element_type=F32)
                for i in range(3)
            )
            loss_ref[m : m + 1, :] = jnp.sum(jnp.where(pick, v, 0.0), axis=0, keepdims=True)

    run_by_time((5.0, scatter2()), (5.0, scatter0()), (5.0, scatter1()), (5.0, loss_order()))

    pad[...] = pltpu.roll(pad[...], lax.rem(FRAME - shift, FRAME), axis=1)
    for m in range(4):
        gh_ref[m] = pad[4 * m : 4 * m + 4, 0:672].astype(BF16)

    for copy in sends:
        copy.wait_send()


def weight_kernel(pt_ref, h_ref, gw_ref):
    cols = pl.ds(pl.multiple_of(pl.program_id(0) * FRAME, 128), FRAME)
    gw_ref[...] = lax.dot_general(
        pt_ref[...], h_ref[:, cols], (((1,), (0,)), ((), ())), preferred_element_type=F32
    ).astype(BF16)


def per_device(final_hidden, out_weight, targets, token_weight):
    vm, dma = pltpu.VMEM, pltpu.SemaphoreType.DMA
    scratch = [
        vm((512, 5376), BF16),
        vm((512, 512), F32),
        vm((512, 512), BF16),
        vm((16, FRAME), F32),
        vm((512, FRAME), F32),
        vm((4, 8, 128), F32),
        vm((1, 512), jnp.int32),
        vm((1, 512), F32),
        vm((2, NX, NZ, NY, 16, LANES), BF16),
        vm((2, NX, NZ, NY, 16, LANES), BF16),
        vm((2, NX, NZ, NY, 16, LANES), BF16),
        vm((NX, 512, FRAME), BF16),
        vm((NX, 512, FRAME), BF16),
        vm((NX, NZ, NY, 16, LANES), BF16),
        vm((NY, NX, NZ, 16, LANES), BF16),
        vm((NZ, NX, NY, 16, LANES), BF16),
        vm((4, NY, 16, LANES), BF16),
        vm((4, NY, 16, LANES), BF16),
        vm((NZ, NY, 16, LANES), BF16),
        vm((NZ, NY, 16, LANES), BF16),
        vm((2, NZ, 16, LANES), BF16),
        vm((2, NZ, 16, LANES), BF16),
        vm((NX, NZ, 16, LANES), BF16),
        vm((NX, NZ, 16, LANES), BF16),
        vm((4, NX, NY, 16, LANES), BF16),
        vm((4, NX, NY, 16, LANES), BF16),
        vm((NY, NZ, 16, LANES), BF16),
        vm((NX, NZ, 16, LANES), BF16),
        vm((NX, NY, 16, LANES), BF16),
        vm((NY - 1, NZ, 16, LANES), BF16),
        vm((NX - 1, NZ, 16, LANES), BF16),
        vm((NX - 1, NY, 16, LANES), BF16),
        vm((NZ, 16, LANES), F32),
        vm((NZ, 16, LANES), F32),
        vm((NY, 16, LANES), F32),
        vm((NZ - 1, 16, LANES), F32),
        vm((NZ - 1, 16, LANES), F32),
        vm((NY - 1, 16, LANES), F32),
        vm((16, 8, 128), F32),
        vm((16, 8, 128), F32),
        dma, dma((COPIES,)), dma((COPIES,)),
    ]
    vmem = pl.BlockSpec(memory_space=pltpu.VMEM)
    hbm = pl.BlockSpec(memory_space=pl.ANY)
    loss, grad_hidden, hidden, grads = pl.pallas_call(
        kernel,
        out_shape=(
            jax.ShapeDtypeStruct((4, 128), F32),
            jax.ShapeDtypeStruct((4, 4, 672), BF16),
            pltpu.VMEM((512, 5376), BF16),
            pltpu.VMEM((512, 512), BF16),
        ),
        in_specs=[vmem, hbm, vmem, vmem],
        out_specs=(vmem, vmem, vmem, vmem),
        scratch_shapes=scratch,
        compiler_params=pltpu.CompilerParams(
            collective_id=0, has_side_effects=True, vmem_limit_bytes=48 * 2**20
        ),
        name="xent",
    )(final_hidden, out_weight, targets, token_weight)
    grads = pltpu.with_memory_space_constraint(grads, pltpu.VMEM)
    hidden = pltpu.with_memory_space_constraint(hidden, pltpu.VMEM)
    grad_weight = pl.pallas_call(
        weight_kernel,
        grid=(7,),
        out_shape=jax.ShapeDtypeStruct((512, 5376), BF16),
        in_specs=[vmem, vmem],
        out_specs=pl.BlockSpec((512, FRAME), lambda k: (0, k)),
        compiler_params=pltpu.CompilerParams(vmem_limit_bytes=12 * 2**20),
        name="weight_grad",
    )(grads, hidden)
    return (loss, grad_hidden, grad_weight)


def solution(mesh):
    in_specs = (P(None, "dp", "section"), P(("dp", "section"), None), P(), P())
    out_specs = (P(), P(None, "dp", "section"), P(("dp", "section"), None))
    return jax.shard_map(
        per_device, mesh=mesh, in_specs=in_specs, out_specs=out_specs, check_vma=False
    )
```

```python
import heapq
import math

import jax
import jax.numpy as jnp
from jax import lax
from jax.experimental import pallas as pl
from jax.experimental.pallas import tpu as pltpu
from jax.sharding import PartitionSpec as P

MESH = pl.DeviceIdType.MESH
F32, BF16 = jnp.float32, jnp.bfloat16
NX, NY, NZ = 4, 4, 8
FRAME = 768
PARTS = 3
LANES = 128
HALVES = 2
TOKENS = 256
REL = (2, 1, 3, 0)
SENDS, GROUPS = 7, 110


def frame_tile(section):
    return (21 * section) // 4


def run_by_time(tasks):
    heap = []
    for k, (start, task) in enumerate(tasks):
        heapq.heappush(heap, (start, k, task))
    while heap:
        _, k, task = heapq.heappop(heap)
        try:
            heapq.heappush(heap, (next(task), k, task))
        except StopIteration:
            pass


def pieces(v):
    hi = v.astype(BF16).astype(F32)
    mid = (v - hi).astype(BF16).astype(F32)
    return hi, mid, v - hi - mid


def kernel(
    h_hbm, w_hbm, tgt_hbm, tw_hbm,
    loss_ref, gh_ref, gw,
    h_ref, tgt_ref, tw_ref, h, pt, w, lt, p, pad, mine, rows, tgt, tw,
    a01, a2,
    gs, rc, s0, s1, s2, u0a, u0b, l0, m0, u1a, u1b, l1, m1, l2, m2,
    t0, t1, t2, q0, q1, q2, c01, c2, d01, d2,
    st1, st2,
    in_sem, send_sem, recv_sem,
):
    dp = lax.axis_index("dp")
    section = lax.axis_index("section")
    z, y = dp // NY, dp % NY
    x, c = section // 2, section % 2
    other = 1 - c

    def at(dz=0, dy=0, dx=0, dc=0):
        return (
            lax.rem(z + dz, NZ) * NY + lax.rem(y + dy, NY),
            lax.rem(x + dx, NX) * 2 + lax.rem(c + dc, 2),
        )

    def zo(o):
        return lax.rem(z + o + NZ, NZ)

    def yo(o):
        return lax.rem(y + o + NY, NY)

    def xo(o):
        return lax.rem(x + o + NX, NX)

    sibling = at(dc=1)
    x_right, x_left = at(dx=1), at(dx=3)
    y_right, y_left = at(dy=1), at(dy=3)
    z_right, z_left = at(dz=1), at(dz=7)

    load_h = pltpu.make_async_copy(h_hbm, h_ref, in_sem.at[0])
    load_tgt = pltpu.make_async_copy(tgt_hbm, tgt_ref, in_sem.at[1])
    load_tw = pltpu.make_async_copy(tw_hbm, tw_ref, in_sem.at[2])
    load_w = pltpu.make_async_copy(w_hbm, w, in_sem.at[3])
    for load in (load_h, load_tgt, load_tw):
        load.start()

    plane = [(k // NX, k % NX) for k in range(1, NX * NY)]
    column = [(k // 2, k % 2) for k in range(1, NZ * 2)]
    barrier = pltpu.get_barrier_semaphore()
    for dy, dx in plane:
        pl.semaphore_signal(barrier, inc=1, device_id=at(dy=dy, dx=dx), device_id_type=MESH)
    for dz, dc in column:
        pl.semaphore_signal(barrier, inc=1, device_id=at(dz=dz, dc=dc), device_id_type=MESH)

    rows[...] = jnp.zeros_like(rows)
    pad[...] = jnp.zeros_like(pad)
    st1[...] = jnp.zeros_like(st1)
    st2[...] = jnp.zeros_like(st2)
    load_h.wait()
    for m in range(4):
        pad[4 * m : 4 * m + 4, 0:672] = h_ref[m].astype(F32)
    shift = lax.rem(section, 4) * 32
    framed = pltpu.roll(pad[...], shift, axis=1)
    for q in range(HALVES):
        v = framed[8 * q : 8 * q + 8]
        packed = [
            jnp.concatenate([v[:, j : j + 128], v[:, j + 128 : j + 256]], axis=0).astype(BF16)
            for j in (0, 256, 512)
        ]
        a01[q, c, x, z, y, :, 0:128] = packed[0]
        a01[q, c, x, z, y, :, 128:256] = packed[1]
        a2[q, c, x, z, y] = packed[2]

    pl.semaphore_wait(barrier, len(plane) + len(column))

    def wait_tiles(sem, tiles, sent):
        r = max(d for d in range(1, 33) if tiles % d == 0 and tiles // d <= 42)
        ref = h.at[pl.ds(0, 16 * r), pl.ds(0, 128 * (tiles // r))]
        copy = pltpu.make_async_remote_copy(
            src_ref=ref, dst_ref=ref, send_sem=sem, recv_sem=sem,
            device_id=sibling, device_id_type=MESH,
        )
        if sent:
            copy.wait_send()
        else:
            copy.wait_recv()

    groups = []
    sends = [0]

    def group():
        groups.append(0)
        return len(groups) - 1

    def send(src, dst, device, g):
        tiles = math.prod(src.shape) * jnp.dtype(src.dtype).itemsize // 4096
        if sends[-1] >= 500 and any(
            sends[-1] % d == 0 and sends[-1] // d <= 42 for d in range(1, 33)
        ):
            sends.append(0)
        groups[g] += tiles
        sends[-1] += tiles
        pltpu.make_async_remote_copy(
            src_ref=src, dst_ref=dst, send_sem=send_sem.at[len(sends) - 1],
            recv_sem=recv_sem.at[g], device_id=device, device_id_type=MESH,
        ).start()

    def arrive(g):
        wait_tiles(recv_sem.at[g], groups[g], False)

    def gather(ref, axis, n):
        g = group()
        for o in range(1, n):
            send(ref, ref, at(**{"d" + axis: o}), g)
        return g

    done = set()

    def finish(name):
        done.add(name)

    from_sibling01 = [group() for _ in range(HALVES)]
    from_sibling2 = [group() for _ in range(HALVES)]

    def gather01(q, t):
        first, second = pl.ds(0, 128), pl.ds(128, 128)

        def pass_on(ref):
            send(ref, ref, sibling, from_sibling01[q])

        def part0(o, half):
            return a01.at[q, c, xo(o), pl.ds(4 * half, 4), :, :, first]

        def part1(o, half):
            return a01.at[q, c, pl.ds(2 * half, 2), :, yo(o), :, second]

        e = gather(a01.at[q, c, x, z, y], "z", NZ)
        yield t[0]
        arrive(e)
        e0 = gather(a01.at[q, c, x, :, y, :, first], "y", NY)
        e1 = gather(a01.at[q, c, x, :, y, :, second], "x", NX)
        yield t[1]
        rings = []
        for e, part, right, left in (
            (e0, part0, x_right, x_left), (e1, part1, y_right, y_left)
        ):
            arrive(e)
            near, far = group(), group()
            rings.append((part, right, left, near, far))
            send(part(0, 0), part(0, 0), right, near)
            send(part(0, 1), part(0, 1), left, near)
            send(part(0, 1), part(0, 1), right, far)
            send(part(0, 0), part(0, 0), left, far)
        pass_on(a01.at[q, c, x, :, :, :, first])
        pass_on(a01.at[q, c, :, :, y, :, second])
        yield t[2]
        last = []
        for part, right, left, near, far in rings:
            arrive(near)
            g = group()
            last.append(g)
            send(part(-1, 0), part(-1, 0), right, g)
            send(part(1, 1), part(1, 1), left, g)
        yield t[3]
        arrive(rings[0][4])
        pass_on(a01.at[q, c, xo(-1), :, :, :, first])
        pass_on(a01.at[q, c, xo(1), :, :, :, first])
        arrive(rings[1][4])
        pass_on(a01.at[q, c, :, :, yo(-1), :, second])
        pass_on(a01.at[q, c, :, :, yo(1), :, second])
        yield t[4]
        arrive(last[0])
        pass_on(a01.at[q, c, xo(2), :, :, :, first])
        arrive(last[1])
        pass_on(a01.at[q, c, :, :, yo(2), :, second])
        finish(("gather01", q))

    def gather2(q, t):
        def pass_on(ref):
            send(ref, ref, sibling, from_sibling2[q])

        def part(o, i):
            return a2.at[q, c, i, zo(o)]

        e = gather(a2.at[q, c, x, z, y], "x", NX)
        yield t[0]
        arrive(e)
        e = gather(a2.at[q, c, :, z, y], "y", NY)
        yield t[1]
        arrive(e)
        hop = [group() for _ in range(NX)]
        for i in range(NX):
            k = NX - 1 - i
            send(part(0, i), part(0, i), z_right, hop[i])
            send(part(0, k), part(0, k), z_left, hop[i])
        pass_on(a2.at[q, c, :, z])
        for o in (1, 2, 3):
            after = [group() for _ in range(NX)] if o < 3 else [group()] * 2
            for i in range(NX):
                yield t[1] + o * t[2] + i * 0.3
                arrive(hop[i])
                k = NX - 1 - i
                if o < 3 or i < 2:
                    send(part(-o, i), part(-o, i), z_right, after[i])
                    send(part(o, k), part(o, k), z_left, after[i])
            hop = after
            pass_on(a2.at[q, c, :, zo(-o)])
            pass_on(a2.at[q, c, :, zo(o)])
        yield t[1] + 4 * t[2] + 0.3
        arrive(hop[0])
        pass_on(a2.at[q, c, :, zo(4)])
        finish(("gather2", q))

    def token_order():
        load_w.start()
        yield 1.0
        load_tgt.wait()
        load_tw.wait()
        t = tgt_ref[...]
        parts = [(t & 63).astype(F32), ((t >> 6) & 63).astype(F32), (t >> 12).astype(F32)]
        parts += list(pieces(tw_ref[...]))
        for i in range(6):
            for m in range(4):
                rows[m, i : i + 1, :] = parts[i][m : m + 1, :]
        src = lax.broadcasted_iota(jnp.int32, (128, 512), 0)
        dst = lax.broadcasted_iota(jnp.int32, (128, 512), 1)
        out = jnp.zeros((8, 512), F32)
        for m in range(4):
            hot = dst == (m // 2) * TOKENS + (src // 4) * 8 + (m % 2) * 4 + src % 4
            out += jnp.dot(
                rows[m].astype(BF16), hot.astype(BF16), preferred_element_type=F32
            )
        number = out[0:1].astype(jnp.int32) + out[1:2].astype(jnp.int32) * 64
        tgt[...] = number + out[2:3].astype(jnp.int32) * 4096
        tw[...] = out[3:4] + out[4:5] + out[5:6]

    first_id = (dp * (NX * 2) + section) * 512

    def combine(buf):
        v = buf[...]
        m = jnp.max(v[:, 0:2], axis=0)
        total = m + jnp.log(jnp.sum(jnp.exp(v[:, 0:2] - m[None]), axis=0))
        return total, jnp.sum(v[:, 2:4], axis=0)

    def frame_part(q, s, tile, zz):
        j, low = tile // 2, (tile % 2) * 8
        if j == 2:
            v = a2[q, s % 2, s // 2, zz]
        else:
            v = a01[q, s % 2, s // 2, zz, :, :, j * 128 : j * 128 + 128]
        return v.astype(F32)[:, low : low + 8].reshape(NY * 8, 128)

    def assemble(q, first, last):
        def step(zz, carry):
            dst = pl.ds(pl.multiple_of(q * TOKENS + zz * 32, 32), 32)
            for tile in range(42):
                v = None
                for s in range(8):
                    if frame_tile(s) <= tile < frame_tile(s) + 6:
                        part = frame_part(q, s, tile - frame_tile(s), zz)
                        v = part if v is None else v + part
                h[dst, tile * 128 : tile * 128 + 128] = v.astype(BF16)
            return carry

        lax.fori_loop(first, last, step, 0)

    def loss_order(q, loss):
        for i, v in enumerate(pieces(loss)):
            rows[i] = jnp.concatenate([v, jnp.zeros((6, 128), F32)], axis=0)
        src = lax.broadcasted_iota(jnp.int32, (128, 128), 0)
        dst = lax.broadcasted_iota(jnp.int32, (128, 128), 1)
        pick = lax.broadcasted_iota(jnp.int32, (8, 128), 0) == (
            lax.broadcasted_iota(jnp.int32, (8, 128), 1) // 64
        )
        for m in (0, 1):
            hot = (src == ((dst // 4) % 16) * 8 + m * 4 + dst % 4).astype(BF16)
            v = sum(
                jnp.dot(rows[i].astype(BF16), hot, preferred_element_type=F32)
                for i in range(3)
            )
            k = 2 * q + m
            loss_ref[k : k + 1, :] = jnp.sum(jnp.where(pick, v, 0.0), axis=0, keepdims=True)

    def share(q, s):
        cols = pl.ds(pl.multiple_of(frame_tile(s) * 128, 128), FRAME)
        return lax.dot_general(
            p[q], w[:, cols], (((1,), (0,)), ((), ())), preferred_element_type=F32
        )

    up, down = pl.ds(0, 4), pl.ds(4, 4)
    up_slice, down_slice = slice(0, 4), slice(4, 8)
    front, back = pl.ds(0, 2), pl.ds(2, 2)
    near0, near1, far0, far1 = ([group() for _ in range(HALVES)] for _ in range(4))
    ring2 = [
        {(k, i): group() for k in (1, 2, 3, 4) for i in range(NX) if k > 1 or i < 2}
        for _ in range(HALVES)
    ]
    tasks = []

    def main(q, t):
        cols = slice(q * TOKENS, q * TOKENS + TOKENS)
        yield t[0]
        assert ("gather01", q) in done and ("gather2", q) in done
        arrive(from_sibling01[q])
        arrive(from_sibling2[q])
        if q == 0:
            load_w.wait()
        for k in range(4):
            assemble(q, 2 * k, 2 * k + 2)
            yield t[0] + 0.4 * (k + 1)
        for k in range(7):
            feats = slice(k * 768, k * 768 + 768)
            v = lax.dot_general(
                w[:, feats], h[cols, feats], (((1,), (1,)), ((), ())),
                preferred_element_type=F32,
            )
            if k == 0:
                lt[q] = v
            else:
                lt[q] += v
            yield t[0] + 1.6 + 0.2 * (k + 1)
        ids = first_id + lax.broadcasted_iota(jnp.int32, (512, TOKENS), 0)
        logits = lt[q]
        picked = jnp.sum(jnp.where(ids == tgt[:, cols], logits, 0.0), axis=0, keepdims=True)
        top = jnp.max(logits, axis=0, keepdims=True)
        lse = top + jnp.log(jnp.sum(jnp.exp(logits - top), axis=0, keepdims=True))
        for i in range(2):
            st1[q, 0, i : i + 1, :] = lse[:, i * 128 : i * 128 + 128]
            st1[q, 0, 2 + i : 3 + i, :] = picked[:, i * 128 : i * 128 + 128]
        around = group()
        for k, d in enumerate(plane):
            send(st1.at[q, 0], st1.at[q, k + 1], at(dy=d[0], dx=d[1]), around)
        yield t[1]
        arrive(around)
        total, hit = combine(st1.at[q])
        st2[q, 0, 0:2, :] = total
        st2[q, 0, 2:4, :] = hit
        around = group()
        for k, d in enumerate(column):
            send(st2.at[q, 0], st2.at[q, k + 1], at(dz=d[0], dc=d[1]), around)
        yield t[2]
        arrive(around)
        log_norm, hit = combine(st2.at[q])
        norm_row = jnp.concatenate([log_norm[i : i + 1] for i in range(2)], axis=1)
        for b in range(4):
            r = slice(b * 128, b * 128 + 128)
            ids = first_id + b * 128 + lax.broadcasted_iota(jnp.int32, (128, TOKENS), 0)
            hot = (ids == tgt[:, cols]).astype(F32)
            g = tw[:, cols] * (jnp.exp(lt[q, r, :] - norm_row) - hot)
            pt[r, cols] = g.astype(BF16)
            p[q, :, r] = jnp.transpose(g).astype(BF16)
        core = []
        for i, o in enumerate(REL):
            gs[q, i] = share(q, xo(o) * 2 + other).astype(BF16)
            core.append(group())
            send(gs.at[q, i], rc.at[q, i], sibling, core[i])
        for i in range(NX):
            yield t[3] + i * 0.7
            mine[...] = share(q, xo(REL[i]) * 2 + c)
            arrive(core[i])
            for zz in range(NZ):
                r = slice(zz * 32, zz * 32 + 32)
                v = mine[r, :] + rc[q, i, r, :].astype(F32)
                for yy in range(NY):
                    u = v[yy * 8 : yy * 8 + 8]
                    packed = [
                        jnp.concatenate(
                            [u[:, j : j + 128], u[:, j + 128 : j + 256]], axis=0
                        ).astype(BF16)
                        for j in (0, 256, 512)
                    ]
                    s0[q, i, zz, yy] = packed[0]
                    s1[q, yy, i, zz] = packed[1]
                    s2[q, zz, i, yy] = packed[2]
            first_sends(q, i)
        loss_order(q, log_norm - hit)
        finish(("main", q))

    def first_sends(q, i):
        if i == 0:
            send(s0.at[q, 0, up], u0a.at[q], x_right, near0[q])
            send(s0.at[q, 0, down], u0b.at[q], x_left, near0[q])
        k = NX - 1 - i
        if i < 2:
            send(s2.at[q, zo(4), i], l2.at[q, 0, i], z_right, ring2[q][1, i])
            send(s2.at[q, zo(-3), i], m2.at[q, 1, i], z_left, ring2[q][2, k])
        else:
            send(s2.at[q, zo(4), i], m2.at[q, 0, i], z_left, ring2[q][1, k])
            send(s2.at[q, zo(3), i], l2.at[q, 1, i], z_right, ring2[q][2, i])
        if i == 1:
            send(s1.at[q, yo(2), front], u1a.at[q], y_right, near1[q])
            send(s1.at[q, yo(-1), front], m1.at[q, front], y_left, far1[q])
            send(s0.at[q, 1, down], l0.at[q, down], x_right, far0[q])
        if i == 2:
            send(s0.at[q, 2, up], m0.at[q, up], x_left, far0[q])
        if i == 3:
            send(s1.at[q, yo(2), back], u1b.at[q], y_left, near1[q])
            send(s1.at[q, yo(1), back], l1.at[q, back], y_right, far1[q])

    def scatter01(q, t):
        yield t[0]
        arrive(near0[q])
        s0[q, 1, up_slice] = (
            s0[q, 1, up_slice].astype(F32) + u0a[q].astype(F32)
        ).astype(BF16)
        send(s0.at[q, 1, up], l0.at[q, up], x_right, far0[q])
        s0[q, 2, down_slice] = (
            s0[q, 2, down_slice].astype(F32) + u0b[q].astype(F32)
        ).astype(BF16)
        send(s0.at[q, 2, down], m0.at[q, down], x_left, far0[q])
        yield t[1]
        assert ("main", q) in done
        arrive(near1[q])
        r = yo(1)
        s1[q, r, 0:2] = (s1[q, r, 0:2].astype(F32) + u1a[q].astype(F32)).astype(BF16)
        send(s1.at[q, r, front], l1.at[q, front], y_right, far1[q])
        r = yo(-1)
        s1[q, r, 2:4] = (s1[q, r, 2:4].astype(F32) + u1b[q].astype(F32)).astype(BF16)
        send(s1.at[q, r, back], m1.at[q, back], y_left, far1[q])
        yield t[2]
        arrive(far0[q])
        for zz in range(NZ):
            v = s0[q, 3, zz].astype(F32) + l0[q, zz].astype(F32) + m0[q, zz].astype(F32)
            v = v.astype(BF16)
            for yy in range(NY):
                t0[q, yy, zz] = v[yy]
        e0 = group()
        for o in range(1, NY):
            send(t0.at[q, yo(o)], q0.at[q, o - 1], at(dy=o), e0)
        yield t[2] + 0.1
        arrive(far1[q])
        for i in range(NX):
            v = s1[q, y, i].astype(F32) + l1[q, i].astype(F32) + m1[q, i].astype(F32)
            t1[q, i] = v.astype(BF16)
        e1 = group()
        for o in range(1, NX):
            send(t1.at[q, REL.index(o)], q1.at[q, o - 1], at(dx=o), e1)
        yield t[3]
        arrive(e0)
        c01[q, :, :, 0:128] = sum(
            [q0[q, k].astype(F32) for k in range(NY - 1)], t0[q, y].astype(F32)
        )
        arrive(e1)
        c01[q, :, :, 128:256] = sum(
            [q1[q, k].astype(F32) for k in range(NX - 1)], t1[q, 3].astype(F32)
        )
        e = group()
        for o in range(1, NZ):
            send(c01.at[q, zo(o)], d01.at[q, o - 1], at(dz=o), e)
        yield t[4]
        arrive(e)
        v = sum([d01[q, k] for k in range(NZ - 1)], c01[q, z])
        r = slice(8 * q, 8 * q + 8)
        pad[r, 0:128] = v[0:8, 0:128]
        pad[r, 128:256] = v[8:16, 0:128]
        pad[r, 256:384] = v[0:8, 128:256]
        pad[r, 384:512] = v[8:16, 128:256]
        finish(("scatter01", q))
        write_hidden(q)

    def scatter2(q, t):
        for k in (1, 2, 3):
            for i in range(NX):
                if k == 1 and i > 1:
                    continue
                yield t[0] + (k - 1) * t[1] + i * 0.3
                assert ("main", q) in done or k == 1
                arrive(ring2[q][k, i])
                j = NX - 1 - i
                r = zo(4 - k)
                v = s2[q, r, i].astype(F32) + l2[q, k - 1, i].astype(F32)
                s2[q, r, i] = v.astype(BF16)
                send(s2.at[q, r, i], l2.at[q, k, i], z_right, ring2[q][k + 1, i])
                r = zo(k - 4)
                v = s2[q, r, j].astype(F32) + m2[q, k - 1, j].astype(F32)
                s2[q, r, j] = v.astype(BF16)
                send(s2.at[q, r, j], m2.at[q, k, j], z_left, ring2[q][k + 1, i])
        yield t[0] + 3 * t[1] + 0.9
        for i in range(NX):
            arrive(ring2[q][4, i])
        for i in range(NX):
            v = s2[q, z, i].astype(F32) + l2[q, 3, i].astype(F32) + m2[q, 3, i].astype(F32)
            t2[q, i] = v.astype(BF16)
        e = group()
        for o in range(1, NX):
            send(t2.at[q, REL.index(o)], q2.at[q, o - 1], at(dx=o), e)
        yield t[2]
        arrive(e)
        c2[q] = sum([q2[q, k].astype(F32) for k in range(NX - 1)], t2[q, 3].astype(F32))
        e = group()
        for o in range(1, NY):
            send(c2.at[q, yo(o)], d2.at[q, o - 1], at(dy=o), e)
        yield t[3]
        arrive(e)
        v = sum([d2[q, k] for k in range(NY - 1)], c2[q, y])
        r = slice(8 * q, 8 * q + 8)
        pad[r, 512:640] = v[0:8]
        pad[r, 640:768] = v[8:16]
        finish(("scatter2", q))
        write_hidden(q)

    def write_hidden(q):
        if ("scatter01", q) in done and ("scatter2", q) in done:
            r = slice(8 * q, 8 * q + 8)
            v = pltpu.roll(pad[r, :], lax.rem(FRAME - shift, FRAME), axis=1)
            pad[r, :] = v
            for m in (0, 1):
                k = 8 * q + 4 * m
                gh_ref[2 * q + m] = pad[k : k + 4, 0:672].astype(BF16)

    def weight(t):
        for k in range(14):
            yield t + 0.7 * k
            assert ("main", 0) in done and ("main", 1) in done
            feats = slice(k * 384, k * 384 + 384)
            gw[:, feats] = lax.dot_general(
                pt[...], h[:, feats], (((1,), (0,)), ((), ())), preferred_element_type=F32
            ).astype(BF16)

    run_by_time(
        [
            (0.0, gather01(0, (4.6, 8.2, 10.7, 12.4, 14.2))),
            (0.1, gather2(0, (2.4, 5.2, 2.5))),
            (0.2, gather01(1, (5.4, 9.2, 12.8, 15.0, 17.0))),
            (0.3, gather2(1, (2.6, 5.6, 2.8))),
            (0.9, token_order()),
            (16.6, main(0, (16.6, 24.3, 28.8, 30.5))),
            (19.0, main(1, (19.0, 27.0, 31.5, 34.0))),
            (34.0, scatter01(0, (34.0, 35.0, 38.0, 42.0, 47.0))),
            (34.0, scatter2(0, (35.0, 2.5, 45.0, 47.5))),
            (37.5, scatter01(1, (37.5, 38.7, 42.5, 46.0, 51.0))),
            (38.0, scatter2(1, (38.6, 2.5, 48.5, 51.0))),
            (38.0, weight(38.0)),
        ]
    )

    for k, tiles in enumerate(sends):
        wait_tiles(send_sem.at[k], tiles, True)
    assert len(sends) == SENDS and len(groups) == GROUPS, (len(sends), len(groups))


def store_kernel(loss, gh, gw, loss_out, gh_out, gw_out, sem):
    copies = [
        pltpu.make_async_copy(loss, loss_out, sem.at[8]),
        pltpu.make_async_copy(gh, gh_out, sem.at[9]),
    ]
    for k in range(8):
        r = pl.ds(64 * k, 64)
        copies.append(pltpu.make_async_copy(gw.at[r], gw_out.at[r], sem.at[k]))
    for copy in copies:
        copy.start()
    for copy in copies:
        copy.wait()


def per_device(final_hidden, out_weight, targets, token_weight):
    vm, dma = pltpu.VMEM, pltpu.SemaphoreType.DMA
    n = HALVES
    scratch = [
        vm((4, 4, 672), BF16),
        vm((4, 128), jnp.int32),
        vm((4, 128), F32),
        vm((512, 5376), BF16),
        vm((512, 512), BF16),
        vm((512, 5376), BF16),
        vm((n, 512, TOKENS), F32),
        vm((n, TOKENS, 512), BF16),
        vm((16, FRAME), F32),
        vm((TOKENS, FRAME), F32),
        vm((4, 8, 128), F32),
        vm((1, 512), jnp.int32),
        vm((1, 512), F32),
        vm((n, 2, NX, NZ, NY, 16, 2 * LANES), BF16),
        vm((n, 2, NX, NZ, NY, 16, LANES), BF16),
        vm((n, NX, TOKENS, FRAME), BF16),
        vm((n, NX, TOKENS, FRAME), BF16),
        vm((n, NX, NZ, NY, 16, LANES), BF16),
        vm((n, NY, NX, NZ, 16, LANES), BF16),
        vm((n, NZ, NX, NY, 16, LANES), BF16),
        vm((n, 4, NY, 16, LANES), BF16),
        vm((n, 4, NY, 16, LANES), BF16),
        vm((n, NZ, NY, 16, LANES), BF16),
        vm((n, NZ, NY, 16, LANES), BF16),
        vm((n, 2, NZ, 16, LANES), BF16),
        vm((n, 2, NZ, 16, LANES), BF16),
        vm((n, NX, NZ, 16, LANES), BF16),
        vm((n, NX, NZ, 16, LANES), BF16),
        vm((n, 4, NX, NY, 16, LANES), BF16),
        vm((n, 4, NX, NY, 16, LANES), BF16),
        vm((n, NY, NZ, 16, LANES), BF16),
        vm((n, NX, NZ, 16, LANES), BF16),
        vm((n, NX, NY, 16, LANES), BF16),
        vm((n, NY - 1, NZ, 16, LANES), BF16),
        vm((n, NX - 1, NZ, 16, LANES), BF16),
        vm((n, NX - 1, NY, 16, LANES), BF16),
        vm((n, NZ, 16, 2 * LANES), F32),
        vm((n, NY, 16, LANES), F32),
        vm((n, NZ - 1, 16, 2 * LANES), F32),
        vm((n, NY - 1, 16, LANES), F32),
        vm((n, 16, 8, 128), F32),
        vm((n, 16, 8, 128), F32),
        dma((4,)), dma((SENDS,)), dma((GROUPS,)),
    ]
    vmem = pl.BlockSpec(memory_space=pltpu.VMEM)
    hbm = pl.BlockSpec(memory_space=pl.ANY)
    final_hidden, targets, token_weight = (
        pltpu.with_memory_space_constraint(v, pltpu.HBM)
        for v in (final_hidden, targets, token_weight)
    )
    loss, grad_hidden, grad_weight = pl.pallas_call(
        kernel,
        out_shape=(
            pltpu.VMEM((4, 128), F32),
            pltpu.VMEM((4, 4, 672), BF16),
            pltpu.VMEM((512, 5376), BF16),
        ),
        in_specs=[hbm, hbm, hbm, hbm],
        out_specs=(vmem, vmem, vmem),
        scratch_shapes=scratch,
        compiler_params=pltpu.CompilerParams(
            collective_id=0, has_side_effects=True, vmem_limit_bytes=48 * 2**20
        ),
        name="xent",
    )(final_hidden, out_weight, targets, token_weight)
    return pl.pallas_call(
        store_kernel,
        out_shape=(
            jax.ShapeDtypeStruct((4, 128), F32),
            jax.ShapeDtypeStruct((4, 4, 672), BF16),
            jax.ShapeDtypeStruct((512, 5376), BF16),
        ),
        in_specs=[vmem, vmem, vmem],
        out_specs=(hbm, hbm, hbm),
        scratch_shapes=[dma((10,))],
        compiler_params=pltpu.CompilerParams(vmem_limit_bytes=2**20),
        name="store",
    )(
        *(
            pltpu.with_memory_space_constraint(v, pltpu.VMEM)
            for v in (loss, grad_hidden, grad_weight)
        )
    )


def solution(mesh):
    in_specs = (P(None, "dp", "section"), P(("dp", "section"), None), P(), P())
    out_specs = (P(), P(None, "dp", "section"), P(("dp", "section"), None))
    return jax.shard_map(
        per_device, mesh=mesh, in_specs=in_specs, out_specs=out_specs, check_vma=False
    )
```

```python
import heapq
import math

import jax
import jax.numpy as jnp
from jax import lax
from jax.experimental import pallas as pl
from jax.experimental.pallas import tpu as pltpu
from jax.sharding import PartitionSpec as P

MESH = pl.DeviceIdType.MESH
F32, BF16 = jnp.float32, jnp.bfloat16
NX, NY, NZ = 4, 4, 8
FRAME = 768
PARTS = 3
LANES = 256
HALVES = 1
TOKENS = 512
REL = (2, 1, 3, 0)
FAR_FIRST = {4: (2, 1, 3), 8: (4, 3, 5, 2, 6, 1, 7)}
SENDS, GROUPS = 4, 71


def frame_tile(section):
    return (21 * section) // 4


def run_by_time(tasks):
    heap = []
    for k, (start, task) in enumerate(tasks):
        heapq.heappush(heap, (start, k, task))
    while heap:
        _, k, task = heapq.heappop(heap)
        try:
            heapq.heappush(heap, (next(task), k, task))
        except StopIteration:
            pass


def pieces(v):
    hi = v.astype(BF16).astype(F32)
    mid = (v - hi).astype(BF16).astype(F32)
    return hi, mid, v - hi - mid


def kernel(
    h_hbm, w_hbm, tgt_hbm, tw_hbm,
    loss_ref, gh_ref, gw,
    h_ref, tgt_ref, tw_ref, h, pt, w, lt, p, pad, mine, rows, tgt, tw,
    a01, a2,
    gs, rc, s0, s1, s2, u0a, u0b, l0, m0, u1a, u1b, l1, m1, l2, m2,
    t0, t1, t2, q0, q1, q2, c0, c1, d0, d1,
    st1, st2,
    in_sem, send_sem, recv_sem,
):
    dp = lax.axis_index("dp")
    section = lax.axis_index("section")
    z, y = dp // NY, dp % NY
    x, c = section // 2, section % 2
    other = 1 - c

    def at(dz=0, dy=0, dx=0, dc=0):
        return (
            lax.rem(z + dz, NZ) * NY + lax.rem(y + dy, NY),
            lax.rem(x + dx, NX) * 2 + lax.rem(c + dc, 2),
        )

    def zo(o):
        return lax.rem(z + o + NZ, NZ)

    def yo(o):
        return lax.rem(y + o + NY, NY)

    def xo(o):
        return lax.rem(x + o + NX, NX)

    sibling = at(dc=1)
    x_right, x_left = at(dx=1), at(dx=3)
    y_right, y_left = at(dy=1), at(dy=3)
    z_right, z_left = at(dz=1), at(dz=7)

    load_h = pltpu.make_async_copy(h_hbm, h_ref, in_sem.at[0])
    load_tgt = pltpu.make_async_copy(tgt_hbm, tgt_ref, in_sem.at[1])
    load_tw = pltpu.make_async_copy(tw_hbm, tw_ref, in_sem.at[2])
    load_w = pltpu.make_async_copy(w_hbm, w, in_sem.at[3])
    for load in (load_h, load_tgt, load_tw):
        load.start()

    def hops(o, n):
        return min(o, n - o)

    plane = [(k // NX, k % NX) for k in range(1, NX * NY)]
    plane.sort(key=lambda d: -hops(d[0], NY) - hops(d[1], NX))
    column = [(k // 2, k % 2) for k in range(1, NZ * 2)]
    column.sort(key=lambda d: -hops(d[0], NZ) - d[1] / 2)
    barrier = pltpu.get_barrier_semaphore()
    for dz, dc in column:
        pl.semaphore_signal(barrier, inc=1, device_id=at(dz=dz, dc=dc), device_id_type=MESH)
    for dy, dx in plane:
        pl.semaphore_signal(barrier, inc=1, device_id=at(dy=dy, dx=dx), device_id_type=MESH)

    rows[...] = jnp.zeros_like(rows)
    pad[...] = jnp.zeros_like(pad)
    st1[...] = jnp.zeros_like(st1)
    st2[...] = jnp.zeros_like(st2)
    load_h.wait()
    for m in range(4):
        pad[4 * m : 4 * m + 4, 0:672] = h_ref[m].astype(F32)
    shift = lax.rem(section, 4) * 32
    framed = pltpu.roll(pad[...], shift, axis=1).astype(BF16)
    a01[0, c, x, z, y] = framed[:, 0:512]
    a2[0, c, x, z, y] = framed[:, 512:768]

    pl.semaphore_wait(barrier, len(plane) + len(column))

    def wait_tiles(sem, tiles, sent):
        r = max(d for d in range(1, 33) if tiles % d == 0 and tiles // d <= 42)
        ref = h.at[pl.ds(0, 16 * r), pl.ds(0, 128 * (tiles // r))]
        copy = pltpu.make_async_remote_copy(
            src_ref=ref, dst_ref=ref, send_sem=sem, recv_sem=sem,
            device_id=sibling, device_id_type=MESH,
        )
        if sent:
            copy.wait_send()
        else:
            copy.wait_recv()

    groups = []
    sends = [0]

    def group():
        groups.append(0)
        return len(groups) - 1

    def send(src, dst, device, g):
        tiles = math.prod(src.shape) * jnp.dtype(src.dtype).itemsize // 4096
        if sends[-1] >= 703 and any(
            sends[-1] % d == 0 and sends[-1] // d <= 42 for d in range(1, 33)
        ):
            sends.append(0)
        groups[g] += tiles
        sends[-1] += tiles
        pltpu.make_async_remote_copy(
            src_ref=src, dst_ref=dst, send_sem=send_sem.at[len(sends) - 1],
            recv_sem=recv_sem.at[g], device_id=device, device_id_type=MESH,
        ).start()

    def arrive(g):
        wait_tiles(recv_sem.at[g], groups[g], False)

    def gather(ref, axis, n):
        g = group()
        for o in FAR_FIRST[n]:
            send(ref, ref, at(**{"d" + axis: o}), g)
        return g

    done = set()

    def finish(name):
        done.add(name)

    from_sibling01 = [group() for _ in range(HALVES)]
    from_sibling2 = [group() for _ in range(HALVES)]

    def gather01(q, t):
        first, second = pl.ds(0, LANES), pl.ds(LANES, LANES)

        def pass_on(ref):
            send(ref, ref, sibling, from_sibling01[q])

        def part0(o, k):
            return a01.at[q, c, xo(o), :, yo(k), :, first]

        def part1(o, k):
            return a01.at[q, c, xo(k), :, yo(o), :, second]

        e = gather(a01.at[q, c, x, z, y], "z", NZ)
        yield t[0]
        arrive(e)
        e0 = gather(a01.at[q, c, x, :, y, :, first], "y", NY)
        e1 = gather(a01.at[q, c, x, :, y, :, second], "x", NX)
        zero0, zero1 = group(), group()
        for part, right, left, zero in (
            (part0, x_right, x_left, zero0), (part1, y_right, y_left, zero1)
        ):
            send(part(0, 0), part(0, 0), right, zero)
            send(part(0, 0), part(0, 0), left, zero)
        yield t[1]
        rings = []
        for e, part, right, left, zero in (
            (e0, part0, x_right, x_left, zero0), (e1, part1, y_right, y_left, zero1)
        ):
            arrive(e)
            near, far, last = group(), group(), group()
            rings.append((part, right, left, near, far, last, zero))
            send(part(0, 1), part(0, 1), right, near)
            send(part(0, 3), part(0, 3), left, near)
            send(part(0, 2), part(0, 2), left, far)
            send(part(0, 2), part(0, 2), right, far)
            send(part(0, 3), part(0, 3), right, far)
            send(part(0, 1), part(0, 1), left, far)
        for part, right, left, near, far, last, zero in rings:
            arrive(zero)
            send(part(-1, 0), part(-1, 0), right, last)
        pass_on(a01.at[q, c, x, :, :, :, first])
        pass_on(a01.at[q, c, :, :, y, :, second])
        yield t[2]
        for part, right, left, near, far, last, zero in rings:
            arrive(near)
            send(part(-1, 1), part(-1, 1), right, last)
            send(part(1, 3), part(1, 3), left, last)
        yield t[3]
        for part, right, left, near, far, last, zero in rings:
            arrive(far)
            send(part(1, 2), part(1, 2), left, last)
        pass_on(a01.at[q, c, xo(-1), :, :, :, first])
        pass_on(a01.at[q, c, xo(1), :, :, :, first])
        pass_on(a01.at[q, c, :, :, yo(-1), :, second])
        pass_on(a01.at[q, c, :, :, yo(1), :, second])
        yield t[4]
        arrive(rings[0][5])
        pass_on(a01.at[q, c, xo(2), :, :, :, first])
        arrive(rings[1][5])
        pass_on(a01.at[q, c, :, :, yo(2), :, second])
        finish(("gather01", q))

    def gather2(q, t):
        def pass_on(ref):
            send(ref, ref, sibling, from_sibling2[q])

        def part(o, i):
            return a2.at[q, c, :, zo(o), yo(i)]

        e = gather(a2.at[q, c, x, z, y], "x", NX)
        yield t[0]
        arrive(e)
        e = gather(a2.at[q, c, :, z, y], "y", NY)
        hop = [group() for _ in range(NY)]
        send(part(0, 0), part(0, 0), z_right, hop[0])
        send(part(0, 0), part(0, 0), z_left, hop[0])
        yield t[1]
        arrive(e)
        for i in (1, 2, 3):
            send(part(0, i), part(0, i), z_right, hop[i])
            send(part(0, i), part(0, i), z_left, hop[i])
        pass_on(a2.at[q, c, :, z])
        for o in (1, 2, 3):
            after = [group() for _ in range(NY)] if o < 3 else [group()] * NY
            for i in range(NY):
                yield t[1] + o * t[2] + i * 0.7 - 0.7
                arrive(hop[i])
                if o < 3 or i < 2:
                    send(part(-o, i), part(-o, i), z_right, after[i])
                if o < 3 or i >= 2:
                    send(part(o, i), part(o, i), z_left, after[i])
            hop = after
            pass_on(a2.at[q, c, :, zo(-o)])
            pass_on(a2.at[q, c, :, zo(o)])
        yield t[1] + 4 * t[2]
        arrive(hop[0])
        pass_on(a2.at[q, c, :, zo(4)])
        finish(("gather2", q))

    def token_order():
        load_w.start()
        yield 1.0
        load_tgt.wait()
        load_tw.wait()
        t = tgt_ref[...]
        parts = [(t & 63).astype(F32), ((t >> 6) & 63).astype(F32), (t >> 12).astype(F32)]
        parts += list(pieces(tw_ref[...]))
        for i in range(6):
            for m in range(4):
                rows[m, i : i + 1, :] = parts[i][m : m + 1, :]
        src = lax.broadcasted_iota(jnp.int32, (128, 512), 0)
        dst = lax.broadcasted_iota(jnp.int32, (128, 512), 1)
        out = jnp.zeros((8, 512), F32)
        for m in range(4):
            hot = dst == (src // 4) * 16 + m * 4 + src % 4
            out += jnp.dot(
                rows[m].astype(BF16), hot.astype(BF16), preferred_element_type=F32
            )
        number = out[0:1].astype(jnp.int32) + out[1:2].astype(jnp.int32) * 64
        tgt[...] = number + out[2:3].astype(jnp.int32) * 4096
        tw[...] = out[3:4] + out[4:5] + out[5:6]

    first_id = (dp * (NX * 2) + section) * 512

    def combine(buf):
        v = buf[...]
        m = jnp.max(v[:, 0:4], axis=0)
        total = m + jnp.log(jnp.sum(jnp.exp(v[:, 0:4] - m[None]), axis=0))
        return total, jnp.sum(v[:, 4:8], axis=0)

    def frame_part(q, s, tile, zz):
        lane = tile * 128
        if tile < 4:
            v = a01[q, s % 2, s // 2, zz, :, :, lane : lane + 128]
        else:
            v = a2[q, s % 2, s // 2, zz, :, :, lane - 512 : lane - 384]
        return v.reshape(NY * 16, 128)

    def assemble(q, first, last):
        def step(zz, carry):
            dst = pl.ds(pl.multiple_of(zz * 64, 64), 64)
            for tile in range(42):
                v = None
                for s in range(8):
                    if frame_tile(s) <= tile < frame_tile(s) + 6:
                        part = frame_part(q, s, tile - frame_tile(s), zz)
                        v = part if v is None else v + part
                h[dst, tile * 128 : tile * 128 + 128] = v
            return carry

        lax.fori_loop(first, last, step, 0)

    def loss_order(q, loss):
        for i, v in enumerate(pieces(loss)):
            rows[i] = jnp.concatenate([v, jnp.zeros((4, 128), F32)], axis=0)
        src = lax.broadcasted_iota(jnp.int32, (128, 128), 0)
        dst = lax.broadcasted_iota(jnp.int32, (128, 128), 1)
        pick = lax.broadcasted_iota(jnp.int32, (8, 128), 0) == (
            lax.broadcasted_iota(jnp.int32, (8, 128), 1) // 32
        )
        for m in range(4):
            hot = (src == ((dst // 4) % 8) * 16 + m * 4 + dst % 4).astype(BF16)
            v = sum(
                jnp.dot(rows[i].astype(BF16), hot, preferred_element_type=F32)
                for i in range(3)
            )
            loss_ref[m : m + 1, :] = jnp.sum(jnp.where(pick, v, 0.0), axis=0, keepdims=True)

    def share(q, s):
        cols = pl.ds(pl.multiple_of(frame_tile(s) * 128, 128), FRAME)
        return lax.dot_general(
            p[q], w[:, cols], (((1,), (0,)), ((), ())), preferred_element_type=F32
        )

    up, down = pl.ds(0, 4), pl.ds(4, 4)
    up_slice, down_slice = slice(0, 4), slice(4, 8)
    front, back = pl.ds(0, 2), pl.ds(2, 2)
    near0, near1, far0, far1 = ([group() for _ in range(HALVES)] for _ in range(4))
    to_right, to_left = (0, 3), (1, 2)
    ring_r = [
        {(k, i): group() for k in (1, 2, 3, 4) for i in range(NX) if k > 1 or i in to_right}
        for _ in range(HALVES)
    ]
    ring_l = [
        {(k, i): group() for k in (1, 2, 3, 4) for i in range(NX) if k > 1 or i in to_left}
        for _ in range(HALVES)
    ]
    tasks = []

    def main(q, t):
        cols = slice(q * TOKENS, q * TOKENS + TOKENS)
        yield t[0]
        assert ("gather01", q) in done and ("gather2", q) in done
        load_w.wait()
        for parity in (c, other):
            if parity is other:
                arrive(from_sibling01[q])
                arrive(from_sibling2[q])
            for xx in range(NX):
                acc = None
                for buf, off, lane in ((a01, 0, 0), (a01, 256, 256), (a2, 0, 512)):
                    feats = frame_tile(2 * xx + parity) * 128 + lane
                    rows_s = buf[q, parity, xx, :, :, :, off : off + LANES]
                    v = lax.dot_general(
                        w[:, pl.ds(pl.multiple_of(feats, 128), LANES)],
                        rows_s.reshape(TOKENS, LANES),
                        (((1,), (1,)), ((), ())), preferred_element_type=F32,
                    )
                    acc = v if acc is None else acc + v
                if parity is c and xx == 0:
                    lt[q] = acc
                else:
                    lt[q] += acc
        ids = first_id + lax.broadcasted_iota(jnp.int32, (512, TOKENS), 0)
        logits = lt[q]
        picked = jnp.sum(jnp.where(ids == tgt[:, cols], logits, 0.0), axis=0, keepdims=True)
        top = jnp.max(logits, axis=0, keepdims=True)
        lse = top + jnp.log(jnp.sum(jnp.exp(logits - top), axis=0, keepdims=True))
        for i in range(4):
            st1[q, 0, i : i + 1, :] = lse[:, i * 128 : i * 128 + 128]
            st1[q, 0, 4 + i : 5 + i, :] = picked[:, i * 128 : i * 128 + 128]
        around = group()
        for k, d in enumerate(plane):
            send(st1.at[q, 0], st1.at[q, k + 1], at(dy=d[0], dx=d[1]), around)
        assemble(q, 0, 4)
        yield t[1]
        arrive(around)
        total, hit = combine(st1.at[q])
        st2[q, 0, 0:4, :] = total
        st2[q, 0, 4:8, :] = hit
        around = group()
        for k, d in enumerate(column):
            send(st2.at[q, 0], st2.at[q, k + 1], at(dz=d[0], dc=d[1]), around)
        assemble(q, 4, 8)
        yield t[2]
        arrive(around)
        log_norm, hit = combine(st2.at[q])
        norm_row = jnp.concatenate([log_norm[i : i + 1] for i in range(4)], axis=1)
        for b in range(4):
            r = slice(b * 128, b * 128 + 128)
            ids = first_id + b * 128 + lax.broadcasted_iota(jnp.int32, (128, TOKENS), 0)
            hot = (ids == tgt[:, cols]).astype(F32)
            g = tw[:, cols] * (jnp.exp(lt[q, r, :] - norm_row) - hot)
            pt[r, cols] = g.astype(BF16)
            p[q, :, r] = jnp.transpose(g).astype(BF16)
        core = []
        for i, o in enumerate(REL):
            gs[q, i] = share(q, xo(o) * 2 + other).astype(BF16)
            core.append(group())
            send(gs.at[q, i], rc.at[q, i], sibling, core[i])
        for i in range(NX):
            yield t[3] + i * 0.7
            mine[...] = share(q, xo(REL[i]) * 2 + c)
            arrive(core[i])
            for zz in range(NZ):
                r = slice(zz * 64, zz * 64 + 64)
                v = (mine[r, :] + rc[q, i, r, :].astype(F32)).astype(BF16)
                s0[q, i, zz] = v[:, 0:256].reshape(NY, 16, LANES)
                for yy in range(NY):
                    s1[q, yy, i, zz] = v[yy * 16 : yy * 16 + 16, 256:512]
                s2[q, zz, i] = v[:, 512:768].reshape(NY, 16, LANES)
            first_sends(q, i)
        loss_order(q, log_norm - hit)
        finish(("main", q))

    def first_sends(q, i):
        if i == 0:
            send(s0.at[q, 0, up], u0a.at[q], x_right, near0[q])
            send(s0.at[q, 0, down], u0b.at[q], x_left, near0[q])
        if i in to_right:
            send(s2.at[q, zo(4), i], l2.at[q, 0, i], z_right, ring_r[q][1, i])
            send(s2.at[q, zo(-3), i], m2.at[q, 1, i], z_left, ring_l[q][2, i])
        else:
            send(s2.at[q, zo(4), i], m2.at[q, 0, i], z_left, ring_l[q][1, i])
            send(s2.at[q, zo(3), i], l2.at[q, 1, i], z_right, ring_r[q][2, i])
        if i == 1:
            send(s1.at[q, yo(2), front], u1a.at[q], y_right, near1[q])
            send(s1.at[q, yo(-1), front], m1.at[q, front], y_left, far1[q])
            send(s0.at[q, 1, down], l0.at[q, down], x_right, far0[q])
        if i == 2:
            send(s0.at[q, 2, up], m0.at[q, up], x_left, far0[q])
        if i == 3:
            send(s1.at[q, yo(2), back], u1b.at[q], y_left, near1[q])
            send(s1.at[q, yo(1), back], l1.at[q, back], y_right, far1[q])

    def scatter0(q, t):
        yield t[0]
        arrive(near0[q])
        s0[q, 1, up_slice] = (
            s0[q, 1, up_slice].astype(F32) + u0a[q].astype(F32)
        ).astype(BF16)
        send(s0.at[q, 1, up], l0.at[q, up], x_right, far0[q])
        s0[q, 2, down_slice] = (
            s0[q, 2, down_slice].astype(F32) + u0b[q].astype(F32)
        ).astype(BF16)
        send(s0.at[q, 2, down], m0.at[q, down], x_left, far0[q])
        yield t[1]
        assert ("main", q) in done
        arrive(far0[q])
        for zz in range(NZ):
            v = s0[q, 3, zz].astype(F32) + l0[q, zz].astype(F32) + m0[q, zz].astype(F32)
            v = v.astype(BF16)
            for yy in range(NY):
                t0[q, yy, zz] = v[yy]
        e = group()
        for o in FAR_FIRST[NY]:
            send(t0.at[q, yo(o)], q0.at[q, o - 1], at(dy=o), e)
        yield t[2]
        arrive(e)
        v = sum([q0[q, k].astype(F32) for k in range(NY - 1)], t0[q, y].astype(F32))
        c0[q] = v.astype(BF16)
        e = group()
        for o in FAR_FIRST[NZ]:
            send(c0.at[q, zo(o)], d0.at[q, o - 1], at(dz=o), e)
        yield t[3]
        arrive(e)
        pad[:, 0:256] = sum(
            [d0[q, k].astype(F32) for k in range(NZ - 1)], c0[q, z].astype(F32)
        )
        finish(("scatter0", q))
        write_hidden(q)

    def scatter1(q, t):
        yield t[0]
        assert ("main", q) in done
        arrive(near1[q])
        r = yo(1)
        s1[q, r, 0:2] = (s1[q, r, 0:2].astype(F32) + u1a[q].astype(F32)).astype(BF16)
        send(s1.at[q, r, front], l1.at[q, front], y_right, far1[q])
        r = yo(-1)
        s1[q, r, 2:4] = (s1[q, r, 2:4].astype(F32) + u1b[q].astype(F32)).astype(BF16)
        send(s1.at[q, r, back], m1.at[q, back], y_left, far1[q])
        yield t[1]
        arrive(far1[q])
        e = group()
        for i, o in enumerate(REL):
            v = s1[q, y, i].astype(F32) + l1[q, i].astype(F32) + m1[q, i].astype(F32)
            t1[q, i] = v.astype(BF16)
            if o:
                send(t1.at[q, i], q1.at[q, o - 1], at(dx=o), e)
        yield t[2]
        arrive(e)
        v = sum([q1[q, k].astype(F32) for k in range(NX - 1)], t1[q, 3].astype(F32))
        c1[q] = v.astype(BF16)
        e = group()
        for o in FAR_FIRST[NZ]:
            send(c1.at[q, zo(o)], d1.at[q, o - 1], at(dz=o), e)
        yield t[3]
        arrive(e)
        pad[:, 256:512] = sum(
            [d1[q, k].astype(F32) for k in range(NZ - 1)], c1[q, z].astype(F32)
        )
        finish(("scatter1", q))
        write_hidden(q)

    def scatter2(q, t, i, moving_right):
        ring = (ring_r if moving_right else ring_l)[q]
        got = l2 if moving_right else m2
        to = z_right if moving_right else z_left
        for k in (1, 2, 3):
            yield t[k - 1]
            if (k, i) not in ring:
                continue
            arrive(ring[k, i])
            r = zo(4 - k) if moving_right else zo(k - 4)
            v = s2[q, r, i].astype(F32) + got[q, k - 1, i].astype(F32)
            s2[q, r, i] = v.astype(BF16)
            send(s2.at[q, r, i], got.at[q, k, i], to, ring[k + 1, i])
        finish(("ring2", i, moving_right))

    def scatter2_end(q, t):
        yield t[0]
        e = group()
        for i in range(NX):
            assert ("ring2", i, True) in done and ("ring2", i, False) in done
            arrive(ring_r[q][4, i])
            arrive(ring_l[q][4, i])
            v = s2[q, z, i].astype(F32) + l2[q, 3, i].astype(F32) + m2[q, 3, i].astype(F32)
            t2[q, i] = v.astype(BF16)
        for k, (dy, dx) in enumerate(plane):
            send(t2.at[q, REL.index(dx), yo(dy)], q2.at[q, k], at(dy=dy, dx=dx), e)
        yield t[1]
        arrive(e)
        pad[:, 512:768] = sum(
            [q2[q, k].astype(F32) for k in range(len(plane))], t2[q, 3, y].astype(F32)
        )
        finish(("scatter2", q))
        write_hidden(q)

    def write_hidden(q):
        if all((name, q) in done for name in ("scatter0", "scatter1", "scatter2")):
            pad[...] = pltpu.roll(pad[...], lax.rem(FRAME - shift, FRAME), axis=1)
            for m in range(4):
                gh_ref[m] = pad[4 * m : 4 * m + 4, 0:672].astype(BF16)

    def weight(t):
        for k in range(14):
            yield t + 0.6 * k
            assert ("main", 0) in done
            feats = slice(k * 384, k * 384 + 384)
            gw[:, feats] = lax.dot_general(
                pt[...], h[:, feats], (((1,), (0,)), ((), ())), preferred_element_type=F32
            ).astype(BF16)

    run_by_time(
        [
            (0.0, gather01(0, (6.0, 10.3, 13.3, 16.3, 19.3))),
            (0.1, gather2(0, (2.6, 6.0, 3.4))),
            (0.9, token_order()),
            (20.0, main(0, (20.0, 27.0, 32.0, 34.0))),
            (39.0, scatter0(0, (39.0, 44.0, 48.5, 53.5))),
            (43.5, scatter1(0, (43.5, 46.7, 51.5, 56.5))),
            (39.1, scatter2(0, (39.1, 41.5, 43.8), 0, True)),
            (41.4, scatter2(0, (41.4, 41.4, 43.7), 0, False)),
            (40.5, scatter2(0, (40.5, 40.5, 42.9), 1, True)),
            (40.6, scatter2(0, (40.6, 42.8, 45.0), 1, False)),
            (42.0, scatter2(0, (42.0, 42.0, 44.3), 2, True)),
            (42.1, scatter2(0, (42.1, 44.4, 46.7), 2, False)),
            (43.3, scatter2(0, (43.3, 45.5, 47.7), 3, True)),
            (43.4, scatter2(0, (43.4, 43.4, 45.6), 3, False)),
            (50.5, scatter2_end(0, (50.5, 55.5))),
            (46.0, weight(46.0)),
        ]
    )

    for k, tiles in enumerate(sends):
        wait_tiles(send_sem.at[k], tiles, True)
    assert len(sends) == SENDS and len(groups) == GROUPS, (len(sends), len(groups))


def store_kernel(loss, gh, gw, loss_out, gh_out, gw_out, sem):
    copies = [
        pltpu.make_async_copy(loss, loss_out, sem.at[8]),
        pltpu.make_async_copy(gh, gh_out, sem.at[9]),
    ]
    for k in range(8):
        r = pl.ds(64 * k, 64)
        copies.append(pltpu.make_async_copy(gw.at[r], gw_out.at[r], sem.at[k]))
    for copy in copies:
        copy.start()
    for copy in copies:
        copy.wait()


def per_device(final_hidden, out_weight, targets, token_weight):
    vm, dma = pltpu.VMEM, pltpu.SemaphoreType.DMA
    n = HALVES
    scratch = [
        vm((4, 4, 672), BF16),
        vm((4, 128), jnp.int32),
        vm((4, 128), F32),
        vm((512, 5376), BF16),
        vm((512, 512), BF16),
        vm((512, 5376), BF16),
        vm((n, 512, TOKENS), F32),
        vm((n, TOKENS, 512), BF16),
        vm((16, FRAME), F32),
        vm((TOKENS, FRAME), F32),
        vm((4, 8, 128), F32),
        vm((1, 512), jnp.int32),
        vm((1, 512), F32),
        vm((n, 2, NX, NZ, NY, 16, 2 * LANES), BF16),
        vm((n, 2, NX, NZ, NY, 16, LANES), BF16),
        vm((n, NX, TOKENS, FRAME), BF16),
        vm((n, NX, TOKENS, FRAME), BF16),
        vm((n, NX, NZ, NY, 16, LANES), BF16),
        vm((n, NY, NX, NZ, 16, LANES), BF16),
        vm((n, NZ, NX, NY, 16, LANES), BF16),
        vm((n, 4, NY, 16, LANES), BF16),
        vm((n, 4, NY, 16, LANES), BF16),
        vm((n, NZ, NY, 16, LANES), BF16),
        vm((n, NZ, NY, 16, LANES), BF16),
        vm((n, 2, NZ, 16, LANES), BF16),
        vm((n, 2, NZ, 16, LANES), BF16),
        vm((n, NX, NZ, 16, LANES), BF16),
        vm((n, NX, NZ, 16, LANES), BF16),
        vm((n, 4, NX, NY, 16, LANES), BF16),
        vm((n, 4, NX, NY, 16, LANES), BF16),
        vm((n, NY, NZ, 16, LANES), BF16),
        vm((n, NX, NZ, 16, LANES), BF16),
        vm((n, NX, NY, 16, LANES), BF16),
        vm((n, NY - 1, NZ, 16, LANES), BF16),
        vm((n, NX - 1, NZ, 16, LANES), BF16),
        vm((n, NX * NY - 1, 16, LANES), BF16),
        vm((n, NZ, 16, LANES), BF16),
        vm((n, NZ, 16, LANES), BF16),
        vm((n, NZ - 1, 16, LANES), BF16),
        vm((n, NZ - 1, 16, LANES), BF16),
        vm((n, 16, 8, 128), F32),
        vm((n, 16, 8, 128), F32),
        dma((4,)), dma((SENDS,)), dma((GROUPS,)),
    ]
    vmem = pl.BlockSpec(memory_space=pltpu.VMEM)
    hbm = pl.BlockSpec(memory_space=pl.ANY)
    final_hidden, targets, token_weight = (
        pltpu.with_memory_space_constraint(v, pltpu.HBM)
        for v in (final_hidden, targets, token_weight)
    )
    loss, grad_hidden, grad_weight = pl.pallas_call(
        kernel,
        out_shape=(
            pltpu.VMEM((4, 128), F32),
            pltpu.VMEM((4, 4, 672), BF16),
            pltpu.VMEM((512, 5376), BF16),
        ),
        in_specs=[hbm, hbm, hbm, hbm],
        out_specs=(vmem, vmem, vmem),
        scratch_shapes=scratch,
        compiler_params=pltpu.CompilerParams(
            collective_id=0, has_side_effects=True, vmem_limit_bytes=48 * 2**20
        ),
        name="xent",
    )(final_hidden, out_weight, targets, token_weight)
    return pl.pallas_call(
        store_kernel,
        out_shape=(
            jax.ShapeDtypeStruct((4, 128), F32),
            jax.ShapeDtypeStruct((4, 4, 672), BF16),
            jax.ShapeDtypeStruct((512, 5376), BF16),
        ),
        in_specs=[vmem, vmem, vmem],
        out_specs=(hbm, hbm, hbm),
        scratch_shapes=[dma((10,))],
        compiler_params=pltpu.CompilerParams(vmem_limit_bytes=2**20),
        name="store",
    )(
        *(
            pltpu.with_memory_space_constraint(v, pltpu.VMEM)
            for v in (loss, grad_hidden, grad_weight)
        )
    )


def solution(mesh):
    in_specs = (P(None, "dp", "section"), P(("dp", "section"), None), P(), P())
    out_specs = (P(), P(None, "dp", "section"), P(("dp", "section"), None))
    return jax.shard_map(
        per_device, mesh=mesh, in_specs=in_specs, out_specs=out_specs, check_vma=False
    )
```

```python
import heapq
import math

import jax
import jax.numpy as jnp
from jax import lax
from jax.experimental import pallas as pl
from jax.experimental.pallas import tpu as pltpu
from jax.sharding import PartitionSpec as P

MESH = pl.DeviceIdType.MESH
F32, BF16 = jnp.float32, jnp.bfloat16
NX, NY, NZ = 4, 4, 8
FRAME = 768
PARTS = 3
LANES = 256
HALVES = 1
TOKENS = 512
REL = (2, 1, 3, 0)
FAR_FIRST = {4: (2, 1, 3), 8: (4, 3, 5, 2, 6, 1, 7)}
SENDS, GROUPS = 4, 71


def frame_tile(section):
    return (21 * section) // 4


def run_by_time(tasks):
    heap = []
    for k, (start, task) in enumerate(tasks):
        heapq.heappush(heap, (start, k, task))
    while heap:
        _, k, task = heapq.heappop(heap)
        try:
            heapq.heappush(heap, (next(task), k, task))
        except StopIteration:
            pass


def pieces(v):
    hi = v.astype(BF16).astype(F32)
    mid = (v - hi).astype(BF16).astype(F32)
    return hi, mid, v - hi - mid


def kernel(
    h_hbm, w_hbm, tgt_hbm, tw_hbm,
    loss_ref, gh_ref, gw,
    h_ref, tgt_ref, tw_ref, h, pt, w, lt, p, pad, mine, rows, tgt, tw,
    a01, a2,
    gs, rc, s0, s1, s2, u0a, u0b, l0, m0, u1a, u1b, l1, m1, l2, m2,
    t0, t1, t2, q0, q1, q2, c0, c1, d0, d1,
    st1, st2,
    in_sem, send_sem, recv_sem,
):
    dp = lax.axis_index("dp")
    section = lax.axis_index("section")
    z, y = dp // NY, dp % NY
    x, c = section // 2, section % 2
    other = 1 - c

    def at(dz=0, dy=0, dx=0, dc=0):
        return (
            lax.rem(z + dz, NZ) * NY + lax.rem(y + dy, NY),
            lax.rem(x + dx, NX) * 2 + lax.rem(c + dc, 2),
        )

    def zo(o):
        return lax.rem(z + o + NZ, NZ)

    def yo(o):
        return lax.rem(y + o + NY, NY)

    def xo(o):
        return lax.rem(x + o + NX, NX)

    sibling = at(dc=1)
    x_right, x_left = at(dx=1), at(dx=3)
    y_right, y_left = at(dy=1), at(dy=3)
    z_right, z_left = at(dz=1), at(dz=7)

    load_h = pltpu.make_async_copy(h_hbm, h_ref, in_sem.at[0])
    load_h.start()

    def hops(o, n):
        return min(o, n - o)

    plane = [(k // NX, k % NX) for k in range(1, NX * NY)]
    plane.sort(key=lambda d: -hops(d[0], NY) - hops(d[1], NX))
    column = [(k // 2, k % 2) for k in range(1, NZ * 2)]
    column.sort(key=lambda d: -hops(d[0], NZ) - d[1] / 2)
    barrier = pltpu.get_barrier_semaphore()
    for dz, dc in column:
        pl.semaphore_signal(barrier, inc=1, device_id=at(dz=dz, dc=dc), device_id_type=MESH)
    for dy, dx in plane:
        pl.semaphore_signal(barrier, inc=1, device_id=at(dy=dy, dx=dx), device_id_type=MESH)

    load_tgt = pltpu.make_async_copy(tgt_hbm, tgt_ref, in_sem.at[1])
    load_tw = pltpu.make_async_copy(tw_hbm, tw_ref, in_sem.at[2])
    load_w = pltpu.make_async_copy(w_hbm, w, in_sem.at[3])
    for load in (load_tgt, load_tw):
        load.start()

    rows[...] = jnp.zeros_like(rows)
    pad[...] = jnp.zeros_like(pad)
    load_h.wait()
    for m in range(4):
        pad[4 * m : 4 * m + 4, 0:672] = h_ref[m].astype(F32)
    shift = lax.rem(section, 4) * 32
    framed = pltpu.roll(pad[...], shift, axis=1).astype(BF16)
    a01[0, c, x, z, y] = framed[:, 0:512]
    a2[0, c, x, z, y] = framed[:, 512:768]

    pl.semaphore_wait(barrier, len(plane) + len(column))

    def wait_tiles(sem, tiles, sent):
        r = max(d for d in range(1, 33) if tiles % d == 0 and tiles // d <= 42)
        ref = h.at[pl.ds(0, 16 * r), pl.ds(0, 128 * (tiles // r))]
        copy = pltpu.make_async_remote_copy(
            src_ref=ref, dst_ref=ref, send_sem=sem, recv_sem=sem,
            device_id=sibling, device_id_type=MESH,
        )
        if sent:
            copy.wait_send()
        else:
            copy.wait_recv()

    groups = []
    sends = [0]

    def group():
        groups.append(0)
        return len(groups) - 1

    def send(src, dst, device, g):
        tiles = math.prod(src.shape) * jnp.dtype(src.dtype).itemsize // 4096
        if sends[-1] >= 703 and any(
            sends[-1] % d == 0 and sends[-1] // d <= 42 for d in range(1, 33)
        ):
            sends.append(0)
        groups[g] += tiles
        sends[-1] += tiles
        pltpu.make_async_remote_copy(
            src_ref=src, dst_ref=dst, send_sem=send_sem.at[len(sends) - 1],
            recv_sem=recv_sem.at[g], device_id=device, device_id_type=MESH,
        ).start()

    def arrive(g):
        wait_tiles(recv_sem.at[g], groups[g], False)

    def gather(ref, axis, n):
        g = group()
        for o in FAR_FIRST[n]:
            send(ref, ref, at(**{"d" + axis: o}), g)
        return g

    done = set()

    def finish(name):
        done.add(name)

    from_sibling01 = [group() for _ in range(HALVES)]
    from_sibling2 = [group() for _ in range(HALVES)]

    def gather01(q, t):
        first, second = pl.ds(0, LANES), pl.ds(LANES, LANES)

        def pass_on(ref):
            send(ref, ref, sibling, from_sibling01[q])

        def part0(o, k):
            return a01.at[q, c, xo(o), :, yo(k), :, first]

        def part1(o, k):
            return a01.at[q, c, xo(k), :, yo(o), :, second]

        e = gather(a01.at[q, c, x, z, y], "z", NZ)
        yield t[0]
        arrive(e)
        e0 = gather(a01.at[q, c, x, :, y, :, first], "y", NY)
        e1 = gather(a01.at[q, c, x, :, y, :, second], "x", NX)
        zero0, zero1 = group(), group()
        for part, right, left, zero in (
            (part0, x_right, x_left, zero0), (part1, y_right, y_left, zero1)
        ):
            send(part(0, 0), part(0, 0), right, zero)
            send(part(0, 0), part(0, 0), left, zero)
        yield t[1]
        rings = []
        for e, part, right, left, zero in (
            (e0, part0, x_right, x_left, zero0), (e1, part1, y_right, y_left, zero1)
        ):
            arrive(e)
            near, far, last = group(), group(), group()
            rings.append((part, right, left, near, far, last, zero))
            send(part(0, 1), part(0, 1), right, near)
            send(part(0, 3), part(0, 3), left, near)
            send(part(0, 2), part(0, 2), left, far)
            send(part(0, 2), part(0, 2), right, far)
            send(part(0, 3), part(0, 3), right, far)
            send(part(0, 1), part(0, 1), left, far)
        for part, right, left, near, far, last, zero in rings:
            arrive(zero)
            send(part(-1, 0), part(-1, 0), right, last)
        pass_on(a01.at[q, c, x, :, :, :, first])
        pass_on(a01.at[q, c, :, :, y, :, second])
        yield t[2]
        for part, right, left, near, far, last, zero in rings:
            arrive(near)
            send(part(-1, 1), part(-1, 1), right, last)
            send(part(1, 3), part(1, 3), left, last)
        yield t[3]
        for part, right, left, near, far, last, zero in rings:
            arrive(far)
            send(part(1, 2), part(1, 2), left, last)
        pass_on(a01.at[q, c, xo(-1), :, :, :, first])
        pass_on(a01.at[q, c, xo(1), :, :, :, first])
        pass_on(a01.at[q, c, :, :, yo(-1), :, second])
        pass_on(a01.at[q, c, :, :, yo(1), :, second])
        yield t[4]
        arrive(rings[0][5])
        pass_on(a01.at[q, c, xo(2), :, :, :, first])
        arrive(rings[1][5])
        pass_on(a01.at[q, c, :, :, yo(2), :, second])
        finish(("gather01", q))

    def gather2(q, t):
        def pass_on(ref):
            send(ref, ref, sibling, from_sibling2[q])

        def part(o, i):
            return a2.at[q, c, :, zo(o), yo(i)]

        e = gather(a2.at[q, c, x, z, y], "x", NX)
        yield t[0]
        arrive(e)
        e = gather(a2.at[q, c, :, z, y], "y", NY)
        hop = [group() for _ in range(NY)]
        send(part(0, 0), part(0, 0), z_right, hop[0])
        send(part(0, 0), part(0, 0), z_left, hop[0])
        yield t[1]
        arrive(e)
        for i in (1, 2, 3):
            send(part(0, i), part(0, i), z_right, hop[i])
            send(part(0, i), part(0, i), z_left, hop[i])
        pass_on(a2.at[q, c, :, z])
        for o in (1, 2, 3):
            after = [group() for _ in range(NY)] if o < 3 else [group()] * NY
            for i in range(NY):
                yield t[1] + o * t[2] + i * 0.7 - 0.7
                arrive(hop[i])
                if o < 3 or i < 2:
                    send(part(-o, i), part(-o, i), z_right, after[i])
                if o < 3 or i >= 2:
                    send(part(o, i), part(o, i), z_left, after[i])
            hop = after
            pass_on(a2.at[q, c, :, zo(-o)])
            pass_on(a2.at[q, c, :, zo(o)])
        yield t[1] + 4 * t[2]
        arrive(hop[0])
        pass_on(a2.at[q, c, :, zo(4)])
        finish(("gather2", q))

    def token_order():
        load_w.start()
        yield 1.0
        load_tgt.wait()
        load_tw.wait()
        t = tgt_ref[...]
        parts = [(t & 63).astype(F32), ((t >> 6) & 63).astype(F32), (t >> 12).astype(F32)]
        parts += list(pieces(tw_ref[...]))
        for i in range(6):
            for m in range(4):
                rows[m, i : i + 1, :] = parts[i][m : m + 1, :]
        src = lax.broadcasted_iota(jnp.int32, (128, 512), 0)
        dst = lax.broadcasted_iota(jnp.int32, (128, 512), 1)
        out = jnp.zeros((8, 512), F32)
        for m in range(4):
            hot = dst == (src // 4) * 16 + m * 4 + src % 4
            out += jnp.dot(
                rows[m].astype(BF16), hot.astype(BF16), preferred_element_type=F32
            )
        number = out[0:1].astype(jnp.int32) + out[1:2].astype(jnp.int32) * 64
        tgt[...] = number + out[2:3].astype(jnp.int32) * 4096
        tw[...] = out[3:4] + out[4:5] + out[5:6]

    first_id = (dp * (NX * 2) + section) * 512

    def combine(buf):
        v = buf[...]
        m = jnp.max(v[:, 0:4], axis=0)
        total = m + jnp.log(jnp.sum(jnp.exp(v[:, 0:4] - m[None]), axis=0))
        return total, jnp.sum(v[:, 4:8], axis=0)

    def frame_part(q, s, tile, zz):
        lane = tile * 128
        if tile < 4:
            v = a01[q, s % 2, s // 2, zz, :, :, lane : lane + 128]
        else:
            v = a2[q, s % 2, s // 2, zz, :, :, lane - 512 : lane - 384]
        return v.reshape(NY * 16, 128)

    def assemble(q, first, last):
        def step(zz, carry):
            dst = pl.ds(pl.multiple_of(zz * 64, 64), 64)
            for tile in range(42):
                v = None
                for s in range(8):
                    if frame_tile(s) <= tile < frame_tile(s) + 6:
                        part = frame_part(q, s, tile - frame_tile(s), zz)
                        v = part if v is None else v + part
                h[dst, tile * 128 : tile * 128 + 128] = v
            return carry

        lax.fori_loop(first, last, step, 0)

    def loss_order(q, loss):
        for i, v in enumerate(pieces(loss)):
            rows[i] = jnp.concatenate([v, jnp.zeros((4, 128), F32)], axis=0)
        src = lax.broadcasted_iota(jnp.int32, (128, 128), 0)
        dst = lax.broadcasted_iota(jnp.int32, (128, 128), 1)
        pick = lax.broadcasted_iota(jnp.int32, (8, 128), 0) == (
            lax.broadcasted_iota(jnp.int32, (8, 128), 1) // 32
        )
        for m in range(4):
            hot = (src == ((dst // 4) % 8) * 16 + m * 4 + dst % 4).astype(BF16)
            v = sum(
                jnp.dot(rows[i].astype(BF16), hot, preferred_element_type=F32)
                for i in range(3)
            )
            loss_ref[m : m + 1, :] = jnp.sum(jnp.where(pick, v, 0.0), axis=0, keepdims=True)

    def share(q, s):
        cols = pl.ds(pl.multiple_of(frame_tile(s) * 128, 128), FRAME)
        return lax.dot_general(
            p[q], w[:, cols], (((1,), (0,)), ((), ())), preferred_element_type=F32
        )

    up, down = pl.ds(0, 4), pl.ds(4, 4)
    up_slice, down_slice = slice(0, 4), slice(4, 8)
    front, back = pl.ds(0, 2), pl.ds(2, 2)
    near0, near1, far0, far1 = ([group() for _ in range(HALVES)] for _ in range(4))
    to_right, to_left = (0, 3), (1, 2)
    ring_r = [
        {(k, i): group() for k in (1, 2, 3, 4) for i in range(NX) if k > 1 or i in to_right}
        for _ in range(HALVES)
    ]
    ring_l = [
        {(k, i): group() for k in (1, 2, 3, 4) for i in range(NX) if k > 1 or i in to_left}
        for _ in range(HALVES)
    ]
    side = {}

    def main(q, t):
        cols = slice(q * TOKENS, q * TOKENS + TOKENS)
        yield t[0]
        assert ("gather01", q) in done and ("gather2", q) in done
        load_w.wait()
        for parity in (c, other):
            if parity is other:
                arrive(from_sibling01[q])
                arrive(from_sibling2[q])
            for xx in range(NX):
                acc = None
                for buf, off, lane in ((a01, 0, 0), (a01, 256, 256), (a2, 0, 512)):
                    feats = frame_tile(2 * xx + parity) * 128 + lane
                    rows_s = buf[q, parity, xx, :, :, :, off : off + LANES]
                    v = lax.dot_general(
                        w[:, pl.ds(pl.multiple_of(feats, 128), LANES)],
                        rows_s.reshape(TOKENS, LANES),
                        (((1,), (1,)), ((), ())), preferred_element_type=F32,
                    )
                    acc = v if acc is None else acc + v
                if parity is c and xx == 0:
                    lt[q] = acc
                else:
                    lt[q] += acc
        ids = first_id + lax.broadcasted_iota(jnp.int32, (512, TOKENS), 0)
        logits = lt[q]
        picked = jnp.sum(jnp.where(ids == tgt[:, cols], logits, 0.0), axis=0, keepdims=True)
        top = jnp.max(logits, axis=0, keepdims=True)
        lse = top + jnp.log(jnp.sum(jnp.exp(logits - top), axis=0, keepdims=True))
        for i in range(4):
            st1[q, 0, i : i + 1, :] = lse[:, i * 128 : i * 128 + 128]
            st1[q, 0, 4 + i : 5 + i, :] = picked[:, i * 128 : i * 128 + 128]
        around = group()
        for k, d in enumerate(plane):
            send(st1.at[q, 0], st1.at[q, k + 1], at(dy=d[0], dx=d[1]), around)
        assemble(q, 0, 4)
        yield t[1]
        arrive(around)
        total, hit = combine(st1.at[q])
        st2[q, 0, 0:4, :] = total
        st2[q, 0, 4:8, :] = hit
        around = group()
        for k, d in enumerate(column):
            send(st2.at[q, 0], st2.at[q, k + 1], at(dz=d[0], dc=d[1]), around)
        assemble(q, 4, 8)
        yield t[2]
        arrive(around)
        log_norm, hit = combine(st2.at[q])
        norm_row = jnp.concatenate([log_norm[i : i + 1] for i in range(4)], axis=1)
        for b in range(4):
            r = slice(b * 128, b * 128 + 128)
            ids = first_id + b * 128 + lax.broadcasted_iota(jnp.int32, (128, TOKENS), 0)
            hot = (ids == tgt[:, cols]).astype(F32)
            g = tw[:, cols] * (jnp.exp(lt[q, r, :] - norm_row) - hot)
            pt[r, cols] = g.astype(BF16)
            p[q, :, r] = jnp.transpose(g).astype(BF16)
        core = []
        for i, o in enumerate(REL):
            gs[q, i] = share(q, xo(o) * 2 + other).astype(BF16)
            core.append(group())
            send(gs.at[q, i], rc.at[q, i], sibling, core[i])
        for i in range(NX):
            yield t[3] + i * 0.7
            mine[...] = share(q, xo(REL[i]) * 2 + c)
            arrive(core[i])
            for zz in range(NZ):
                r = slice(zz * 64, zz * 64 + 64)
                v = (mine[r, :] + rc[q, i, r, :].astype(F32)).astype(BF16)
                s0[q, i, zz] = v[:, 0:256].reshape(NY, 16, LANES)
                for yy in range(NY):
                    s1[q, yy, i, zz] = v[yy * 16 : yy * 16 + 16, 256:512]
                s2[q, zz, i] = v[:, 512:768].reshape(NY, 16, LANES)
            first_sends(q, i)
        side["loss"] = log_norm - hit
        finish(("main", q))

    def first_sends(q, i):
        if i == 0:
            send(s0.at[q, 0, up], u0a.at[q], x_right, near0[q])
            send(s0.at[q, 0, down], u0b.at[q], x_left, near0[q])
        if i in to_right:
            send(s2.at[q, zo(4), i], l2.at[q, 0, i], z_right, ring_r[q][1, i])
            send(s2.at[q, zo(-3), i], m2.at[q, 1, i], z_left, ring_l[q][2, i])
        else:
            send(s2.at[q, zo(4), i], m2.at[q, 0, i], z_left, ring_l[q][1, i])
            send(s2.at[q, zo(3), i], l2.at[q, 1, i], z_right, ring_r[q][2, i])
        if i == 1:
            send(s1.at[q, yo(2), front], u1a.at[q], y_right, near1[q])
            send(s1.at[q, yo(-1), front], m1.at[q, front], y_left, far1[q])
            send(s0.at[q, 1, down], l0.at[q, down], x_right, far0[q])
        if i == 2:
            send(s0.at[q, 2, up], m0.at[q, up], x_left, far0[q])
        if i == 3:
            send(s1.at[q, yo(2), back], u1b.at[q], y_left, near1[q])
            send(s1.at[q, yo(1), back], l1.at[q, back], y_right, far1[q])

    def scatter0(q, t):
        yield t[0]
        arrive(near0[q])
        s0[q, 1, up_slice] = (
            s0[q, 1, up_slice].astype(F32) + u0a[q].astype(F32)
        ).astype(BF16)
        send(s0.at[q, 1, up], l0.at[q, up], x_right, far0[q])
        s0[q, 2, down_slice] = (
            s0[q, 2, down_slice].astype(F32) + u0b[q].astype(F32)
        ).astype(BF16)
        send(s0.at[q, 2, down], m0.at[q, down], x_left, far0[q])
        yield t[1]
        assert ("main", q) in done
        arrive(far0[q])
        for zz in range(NZ):
            v = s0[q, 3, zz].astype(F32) + l0[q, zz].astype(F32) + m0[q, zz].astype(F32)
            v = v.astype(BF16)
            for yy in range(NY):
                t0[q, yy, zz] = v[yy]
        e = group()
        for o in FAR_FIRST[NY]:
            send(t0.at[q, yo(o)], q0.at[q, o - 1], at(dy=o), e)
        yield t[2]
        arrive(e)
        v = sum([q0[q, k].astype(F32) for k in range(NY - 1)], t0[q, y].astype(F32))
        c0[q] = v.astype(BF16)
        e = group()
        for o in FAR_FIRST[NZ]:
            send(c0.at[q, zo(o)], d0.at[q, o - 1], at(dz=o), e)
        yield t[3]
        arrive(e)
        pad[:, 0:256] = sum(
            [d0[q, k].astype(F32) for k in range(NZ - 1)], c0[q, z].astype(F32)
        )
        finish(("scatter0", q))
        write_hidden(q)

    def scatter1(q, t):
        yield t[0]
        assert ("main", q) in done
        arrive(near1[q])
        r = yo(1)
        s1[q, r, 0:2] = (s1[q, r, 0:2].astype(F32) + u1a[q].astype(F32)).astype(BF16)
        send(s1.at[q, r, front], l1.at[q, front], y_right, far1[q])
        r = yo(-1)
        s1[q, r, 2:4] = (s1[q, r, 2:4].astype(F32) + u1b[q].astype(F32)).astype(BF16)
        send(s1.at[q, r, back], m1.at[q, back], y_left, far1[q])
        yield t[1]
        arrive(far1[q])
        e = group()
        for i, o in enumerate(REL):
            v = s1[q, y, i].astype(F32) + l1[q, i].astype(F32) + m1[q, i].astype(F32)
            t1[q, i] = v.astype(BF16)
            if o:
                send(t1.at[q, i], q1.at[q, o - 1], at(dx=o), e)
        yield t[2]
        arrive(e)
        v = sum([q1[q, k].astype(F32) for k in range(NX - 1)], t1[q, 3].astype(F32))
        c1[q] = v.astype(BF16)
        e = group()
        for o in FAR_FIRST[NZ]:
            send(c1.at[q, zo(o)], d1.at[q, o - 1], at(dz=o), e)
        yield t[3]
        arrive(e)
        pad[:, 256:512] = sum(
            [d1[q, k].astype(F32) for k in range(NZ - 1)], c1[q, z].astype(F32)
        )
        finish(("scatter1", q))
        write_hidden(q)

    def scatter2(q, t, i, moving_right):
        ring = (ring_r if moving_right else ring_l)[q]
        got = l2 if moving_right else m2
        to = z_right if moving_right else z_left
        for k in (1, 2, 3):
            yield t[k - 1]
            if (k, i) not in ring:
                continue
            arrive(ring[k, i])
            r = zo(4 - k) if moving_right else zo(k - 4)
            v = s2[q, r, i].astype(F32) + got[q, k - 1, i].astype(F32)
            s2[q, r, i] = v.astype(BF16)
            send(s2.at[q, r, i], got.at[q, k, i], to, ring[k + 1, i])
        finish(("ring2", i, moving_right))

    def scatter2_end(q, t):
        yield t[0]
        e = group()
        for i in range(NX):
            assert ("ring2", i, True) in done and ("ring2", i, False) in done
            arrive(ring_r[q][4, i])
            arrive(ring_l[q][4, i])
            v = s2[q, z, i].astype(F32) + l2[q, 3, i].astype(F32) + m2[q, 3, i].astype(F32)
            t2[q, i] = v.astype(BF16)
        for k, (dy, dx) in enumerate(plane):
            send(t2.at[q, REL.index(dx), yo(dy)], q2.at[q, k], at(dy=dy, dx=dx), e)
        yield t[1]
        arrive(e)
        pad[:, 512:768] = sum(
            [q2[q, k].astype(F32) for k in range(len(plane))], t2[q, 3, y].astype(F32)
        )
        finish(("scatter2", q))
        write_hidden(q)

    def write_hidden(q):
        if all((name, q) in done for name in ("scatter0", "scatter1", "scatter2")):
            pad[...] = pltpu.roll(pad[...], lax.rem(FRAME - shift, FRAME), axis=1)
            for m in range(4):
                gh_ref[m] = pad[4 * m : 4 * m + 4, 0:672].astype(BF16)

    def write_loss(t):
        yield t
        loss_order(0, side["loss"])

    def weight(t):
        for k in range(14):
            yield t + 0.5 * k
            assert ("main", 0) in done
            feats = slice(k * 384, k * 384 + 384)
            gw[:, feats] = lax.dot_general(
                pt[...], h[:, feats], (((1,), (0,)), ((), ())), preferred_element_type=F32
            ).astype(BF16)

    run_by_time(
        [
            (0.05, gather01(0, (6.0, 10.3, 13.3, 16.3, 19.3))),
            (0.0, gather2(0, (2.6, 6.0, 3.4))),
            (0.9, token_order()),
            (20.0, main(0, (20.0, 27.0, 32.0, 34.0))),
            (39.0, scatter0(0, (39.0, 44.0, 48.5, 53.5))),
            (43.5, scatter1(0, (43.5, 46.7, 51.5, 56.5))),
            (39.1, scatter2(0, (39.1, 41.5, 43.8), 0, True)),
            (41.4, scatter2(0, (41.4, 41.4, 43.7), 0, False)),
            (40.5, scatter2(0, (40.5, 40.5, 42.9), 1, True)),
            (40.6, scatter2(0, (40.6, 42.8, 45.0), 1, False)),
            (42.0, scatter2(0, (42.0, 42.0, 44.3), 2, True)),
            (42.1, scatter2(0, (42.1, 44.4, 46.7), 2, False)),
            (43.3, scatter2(0, (43.3, 45.5, 47.7), 3, True)),
            (43.4, scatter2(0, (43.4, 43.4, 45.6), 3, False)),
            (50.5, scatter2_end(0, (50.5, 55.5))),
            (48.6, weight(48.6)),
            (48.7, write_loss(48.7)),
        ]
    )

    for k, tiles in enumerate(sends):
        wait_tiles(send_sem.at[k], tiles, True)
    assert len(sends) == SENDS and len(groups) == GROUPS, (len(sends), len(groups))


def store_kernel(loss, gh, gw, loss_out, gh_out, gw_out, sem):
    copies = [
        pltpu.make_async_copy(loss, loss_out, sem.at[8]),
        pltpu.make_async_copy(gh, gh_out, sem.at[9]),
    ]
    for k in range(8):
        r = pl.ds(64 * k, 64)
        copies.append(pltpu.make_async_copy(gw.at[r], gw_out.at[r], sem.at[k]))
    for copy in copies:
        copy.start()
    for copy in copies:
        copy.wait()


def per_device(final_hidden, out_weight, targets, token_weight):
    vm, dma = pltpu.VMEM, pltpu.SemaphoreType.DMA
    n = HALVES
    scratch = [
        vm((4, 4, 672), BF16),
        vm((4, 128), jnp.int32),
        vm((4, 128), F32),
        vm((512, 5376), BF16),
        vm((512, 512), BF16),
        vm((512, 5376), BF16),
        vm((n, 512, TOKENS), F32),
        vm((n, TOKENS, 512), BF16),
        vm((16, FRAME), F32),
        vm((TOKENS, FRAME), F32),
        vm((4, 8, 128), F32),
        vm((1, 512), jnp.int32),
        vm((1, 512), F32),
        vm((n, 2, NX, NZ, NY, 16, 2 * LANES), BF16),
        vm((n, 2, NX, NZ, NY, 16, LANES), BF16),
        vm((n, NX, TOKENS, FRAME), BF16),
        vm((n, NX, TOKENS, FRAME), BF16),
        vm((n, NX, NZ, NY, 16, LANES), BF16),
        vm((n, NY, NX, NZ, 16, LANES), BF16),
        vm((n, NZ, NX, NY, 16, LANES), BF16),
        vm((n, 4, NY, 16, LANES), BF16),
        vm((n, 4, NY, 16, LANES), BF16),
        vm((n, NZ, NY, 16, LANES), BF16),
        vm((n, NZ, NY, 16, LANES), BF16),
        vm((n, 2, NZ, 16, LANES), BF16),
        vm((n, 2, NZ, 16, LANES), BF16),
        vm((n, NX, NZ, 16, LANES), BF16),
        vm((n, NX, NZ, 16, LANES), BF16),
        vm((n, 4, NX, NY, 16, LANES), BF16),
        vm((n, 4, NX, NY, 16, LANES), BF16),
        vm((n, NY, NZ, 16, LANES), BF16),
        vm((n, NX, NZ, 16, LANES), BF16),
        vm((n, NX, NY, 16, LANES), BF16),
        vm((n, NY - 1, NZ, 16, LANES), BF16),
        vm((n, NX - 1, NZ, 16, LANES), BF16),
        vm((n, NX * NY - 1, 16, LANES), BF16),
        vm((n, NZ, 16, LANES), BF16),
        vm((n, NZ, 16, LANES), BF16),
        vm((n, NZ - 1, 16, LANES), BF16),
        vm((n, NZ - 1, 16, LANES), BF16),
        vm((n, 16, 8, 128), F32),
        vm((n, 16, 8, 128), F32),
        dma((4,)), dma((SENDS,)), dma((GROUPS,)),
    ]
    vmem = pl.BlockSpec(memory_space=pltpu.VMEM)
    hbm = pl.BlockSpec(memory_space=pl.ANY)
    final_hidden, targets, token_weight = (
        pltpu.with_memory_space_constraint(v, pltpu.HBM)
        for v in (final_hidden, targets, token_weight)
    )
    loss, grad_hidden, grad_weight = pl.pallas_call(
        kernel,
        out_shape=(
            pltpu.VMEM((4, 128), F32),
            pltpu.VMEM((4, 4, 672), BF16),
            pltpu.VMEM((512, 5376), BF16),
        ),
        in_specs=[hbm, hbm, hbm, hbm],
        out_specs=(vmem, vmem, vmem),
        scratch_shapes=scratch,
        compiler_params=pltpu.CompilerParams(
            collective_id=0, has_side_effects=True, vmem_limit_bytes=48 * 2**20
        ),
        name="xent",
    )(final_hidden, out_weight, targets, token_weight)
    return pl.pallas_call(
        store_kernel,
        out_shape=(
            jax.ShapeDtypeStruct((4, 128), F32),
            jax.ShapeDtypeStruct((4, 4, 672), BF16),
            jax.ShapeDtypeStruct((512, 5376), BF16),
        ),
        in_specs=[vmem, vmem, vmem],
        out_specs=(hbm, hbm, hbm),
        scratch_shapes=[dma((10,))],
        compiler_params=pltpu.CompilerParams(vmem_limit_bytes=2**20),
        name="store",
    )(
        *(
            pltpu.with_memory_space_constraint(v, pltpu.VMEM)
            for v in (loss, grad_hidden, grad_weight)
        )
    )


def solution(mesh):
    in_specs = (P(None, "dp", "section"), P(("dp", "section"), None), P(), P())
    out_specs = (P(), P(None, "dp", "section"), P(("dp", "section"), None))
    return jax.shard_map(
        per_device, mesh=mesh, in_specs=in_specs, out_specs=out_specs, check_vma=False
    )
```
